512 devices in a mesh: rep: 4 (over x), grp: 8 (over y), exp: 16 (over z, core).
Axes of the slice: x: 4, y: 8, z: 8, core: 2. Of those that a mesh axis runs over, the one named last changes fastest.
Arguments:
- tokens: bfloat16 [16384, 2048], P(('rep', 'grp', 'exp')), may hold values from -6 to 6
- out_grad: bfloat16 [16384, 2048], P(('rep', 'grp', 'exp')), may hold values from -6 to 6
- gate_prob: float32 [16384, 8], P(('rep', 'grp', 'exp')), may hold values from 0.05 to 0.5
- routes: int32 [16384, 8], P(('rep', 'grp', 'exp')), may hold values from 0 to 127, as said below
- limits: int32 [128], replicated, may hold values from 2 to 3, as said below
- w_gate: bfloat16 [128, 2048, 768], P(('grp', 'exp'), 'rep'), may hold values from -0.125 to 0.125
- w_up: bfloat16 [128, 2048, 768], P(('grp', 'exp'), 'rep'), may hold values from -0.125 to 0.125
- w_down: bfloat16 [128, 768, 2048], P(('grp', 'exp'), None, 'rep'), may hold values from -0.21875 to 0.21875
- up_in: bfloat16 [128, 32, 2048], P(('grp', 'exp')), may hold values from -0.125 to 0.125
- up_out: bfloat16 [128, 32, 768], P(('grp', 'exp')), may hold values from -0.25 to 0.25
- down_in: bfloat16 [128, 32, 768], P(('grp', 'exp')), may hold values from -0.21875 to 0.21875
- down_out: bfloat16 [128, 32, 2048], P(('grp', 'exp')), may hold values from -0.25 to 0.25
Outputs:
- token_grad: bfloat16 [16384, 2048], P(('rep', 'grp', 'exp'))
- up_in_grad: float32 [128, 32, 2048], P(('grp', 'exp'))
- up_out_grad: float32 [128, 32, 768], P(('grp', 'exp'))
- down_in_grad: float32 [128, 32, 768], P(('grp', 'exp'))
- down_out_grad: float32 [128, 32, 2048], P(('grp', 'exp'))
The draws below stay inside these ranges and needn't reach their ends.
Inputs may be any that keep to these rules, and one draw needn't show every extreme that they name: `routes`: each row names 8 different experts, all in at most 4 groups of 16 consecutive experts. The first 3 tokens of every source block name one common expert, whose limit is 3. `limits`: at least one expert has the limit 3.
All inputs are finite; a program needn't handle non-finite values.
Results may differ from the reference program's by a relative error of at most 0.014.
Values may be sent and summed in bfloat16 or wider, within the bound.
No kernel may reach another device: no remote copies, remote signals or barrier semaphores. Data moves between devices by JAX's collectives and lax.ppermute only.
A program may use at most 64 MiB of HBM per device.

```python
import math
import jax
import jax.numpy as jnp
from jax import lax

D = 2048
H = 768
R = 32
TOPK = 8
CAP = 3
TOK_DEV = 32
GROUPS = 8
GROUP_SIZE = 16
EXPERTS = 128
GROUPS_KEPT = 4
REPLICAS = 4
TOKENS = 16384


def full_expert(key):
    return jax.random.randint(key, (), 0, EXPERTS)


def draw_limits(key, part):
    chosen = full_expert(key)
    key = jax.random.fold_in(key, 11)
    values = jax.random.randint(key, (EXPERTS,), CAP - 1, CAP + 1)
    return jnp.where(jnp.arange(EXPERTS) == chosen, CAP, values).astype(jnp.int32)


def draw_routes(key, part):
    chosen = full_expert(key)
    key = jax.random.fold_in(key, 12)
    split_keys = jax.random.split(key, 4)
    favour = jax.random.randint(split_keys[0], (EXPERTS,), 0, 128)
    group_favour = jax.random.randint(split_keys[1], (GROUPS,), 0, 128)
    group_ids = jnp.arange(GROUPS, dtype=jnp.int32)
    expert_ids = jnp.arange(EXPERTS, dtype=jnp.int32)
    forced = (jnp.arange(TOKENS) % TOK_DEV < CAP)[:, None]
    group_score = jax.random.randint(split_keys[2], (TOKENS, GROUPS), 0, 256) + group_favour[None, :]
    group_score = jnp.where(forced & (group_ids[None, :] == chosen // GROUP_SIZE), 1024, group_score)
    group_score = group_score * GROUPS + group_ids[None, :]
    unused, picked = lax.top_k(group_score, GROUPS_KEPT)
    allowed = jnp.any(picked[:, :, None] == group_ids[None, None, :], axis=1)
    allowed_experts = allowed[:, expert_ids // GROUP_SIZE]
    expert_score = jax.random.randint(split_keys[3], (TOKENS, EXPERTS), 0, 256) + favour[None, :]
    expert_score = jnp.where(forced & (expert_ids[None, :] == chosen), 1024, expert_score)
    expert_score = expert_score * EXPERTS + expert_ids[None, :]
    expert_score = jnp.where(allowed_experts, expert_score, -1)
    unused_two, chosen_routes = lax.top_k(expert_score, TOPK)
    return chosen_routes.astype(jnp.int32)


def level_of(stream_key, dims, shards, least, largest):
    level = 1.0
    for position, blocks in shards:
        heights = jax.random.uniform(jax.random.fold_in(jax.random.fold_in(stream_key, 6), position), (blocks,), jnp.float32, least / len(shards), largest / len(shards))
        level = level * jnp.repeat(jnp.exp(heights), dims[position] // blocks).reshape((-1,) + (1,) * (len(dims) - 1 - position))
    return level


def noise(own_key, dims, deviation, bound, cuts=(), kind=jnp.bfloat16):
    values = jax.random.normal(own_key, dims, jnp.float32) * deviation
    if len(cuts) > 0:
        values = level_of(own_key, dims, cuts, -0.22, 0.18) * values
    return jnp.clip(values, min=-bound, max=bound).astype(kind)


def setup_inputs(seed: int = 0) -> dict:
    arg_keys = jax.random.split(jax.random.key(seed), 13)
    tokens = noise(arg_keys[0], (TOKENS, D), 1.0, 6.0, ((0, 512),))
    out_grad = noise(arg_keys[1], (TOKENS, D), 1.0, 6.0, ((0, 512),))
    gate_prob = jnp.clip(jnp.exp(math.log(0.5) - 2.3025851 * jax.random.uniform(arg_keys[2], (TOKENS, TOPK), jnp.float32) ** level_of(arg_keys[2], (TOKENS, TOPK), ((0, 512),), -0.2, 0.2)), 0.05, 0.5)
    routes = draw_routes(jax.random.fold_in(arg_keys[12], 71), 0)
    limits = draw_limits(jax.random.fold_in(arg_keys[12], 71), 0)
    w_gate = noise(arg_keys[5], (EXPERTS, D, H), D ** -0.5, 0.125, ((0, 128), (1, 4)))
    w_up = noise(arg_keys[6], (EXPERTS, D, H), D ** -0.5, 0.125, ((0, 128), (1, 4)))
    w_down = noise(arg_keys[7], (EXPERTS, H, D), H ** -0.5, 0.21875, ((0, 128), (2, 4)))
    up_in = noise(arg_keys[8], (EXPERTS, R, D), D ** -0.5, 0.125, ((0, 128),))
    up_out = noise(arg_keys[9], (EXPERTS, R, H), (16 * R) ** -0.5, 0.25, ((0, 128),))
    down_in = noise(arg_keys[10], (EXPERTS, R, H), H ** -0.5, 0.21875, ((0, 128),))
    down_out = noise(arg_keys[11], (EXPERTS, R, D), (16 * R) ** -0.5, 0.25, ((0, 128),))
    return {"tokens": tokens, "out_grad": out_grad, "gate_prob": gate_prob, "routes": routes, "limits": limits, "w_gate": w_gate, "w_up": w_up, "w_down": w_down, "up_in": up_in, "up_out": up_out, "down_in": down_in, "down_out": down_out}


ADAPTER_SCALE = 2.0


def gated_product(left_side, right_side, left_dim, right_dim):
    left_side = lax.optimization_barrier(left_side).astype(jnp.float32)
    right_side = lax.optimization_barrier(right_side).astype(jnp.float32)
    return lax.dot_general(left_side, right_side, (((left_dim,), (right_dim,)), ((), ())), precision=lax.Precision.HIGHEST)


def expert_backward_pass(input_rows, row_gradient, gate_weight, up_weight, down_weight, adapter_up_input, adapter_up_output, adapter_down_input, adapter_down_output):
    low_rank_up = gated_product(input_rows, adapter_up_input, 1, 1).astype(jnp.bfloat16)
    gate_pre = gated_product(input_rows, gate_weight, 1, 0)
    up_total_sum = gated_product(input_rows, up_weight, 1, 0) + ADAPTER_SCALE * gated_product(low_rank_up, adapter_up_output, 1, 0)
    sigmoid_gate = jax.nn.sigmoid(gate_pre)
    active = gate_pre * sigmoid_gate
    hidden_state = (active * up_total_sum).astype(jnp.bfloat16)
    low_rank_down = gated_product(hidden_state, adapter_down_input, 1, 1).astype(jnp.bfloat16)
    down_output_gradient = ADAPTER_SCALE * gated_product(low_rank_down, row_gradient, 0, 0)
    backward_low_rank = gated_product(row_gradient, adapter_down_output, 1, 1).astype(jnp.bfloat16)
    down_input_gradient = ADAPTER_SCALE * gated_product(backward_low_rank, hidden_state, 0, 0)
    hidden_gradient = gated_product(row_gradient, down_weight, 1, 1) + ADAPTER_SCALE * gated_product(backward_low_rank, adapter_down_input, 1, 0)
    gate_gradient = (hidden_gradient * up_total_sum * sigmoid_gate * (1.0 + gate_pre * (1.0 - sigmoid_gate))).astype(jnp.bfloat16)
    up_gradient = (hidden_gradient * active).astype(jnp.bfloat16)
    up_output_gradient = ADAPTER_SCALE * gated_product(low_rank_up, up_gradient, 0, 0)
    up_low_rank = gated_product(up_gradient, adapter_up_output, 1, 1).astype(jnp.bfloat16)
    up_input_gradient = ADAPTER_SCALE * gated_product(up_low_rank, input_rows, 0, 0)
    slot_gradient = (gated_product(gate_gradient, gate_weight, 1, 1) + gated_product(up_gradient, up_weight, 1, 1) + ADAPTER_SCALE * gated_product(up_low_rank, adapter_up_input, 1, 0)).astype(jnp.bfloat16)
    return slot_gradient, up_input_gradient, up_output_gradient, down_input_gradient, down_output_gradient


def one_expert(items):
    return expert_backward_pass(*items)


def reference(tokens, out_grad, gate_prob, routes, limits, w_gate, w_up, w_down, up_in, up_out, down_in, down_out):
    block_pairs = TOK_DEV * TOPK
    rows_rep = TOK_DEV * EXPERTS
    slot_rows = EXPERTS * CAP
    buffer_rows = EXPERTS * slot_rows
    expert_ids = jnp.arange(EXPERTS, dtype=jnp.int32)
    grad_sums = [jnp.zeros((EXPERTS, R, D), jnp.float32), jnp.zeros((EXPERTS, R, H), jnp.float32), jnp.zeros((EXPERTS, R, H), jnp.float32), jnp.zeros((EXPERTS, R, D), jnp.float32)]
    pieces = []
    for replica in range(REPLICAS):
        rep_tokens = tokens[replica * rows_rep:(replica + 1) * rows_rep]
        rep_grad = out_grad[replica * rows_rep:(replica + 1) * rows_rep]
        rep_prob = gate_prob[replica * rows_rep:(replica + 1) * rows_rep].reshape(-1)
        rep_routes = routes[replica * rows_rep:(replica + 1) * rows_rep].reshape(EXPERTS, block_pairs)
        onehot = (rep_routes[:, :, None] == expert_ids[None, None, :]).astype(jnp.int32)
        slot_rank = jnp.sum((jnp.cumsum(onehot, axis=1) - 1) * onehot, axis=2)
        kept_pair = slot_rank < limits[rep_routes]
        source = jnp.arange(EXPERTS, dtype=jnp.int32)[:, None]
        where_to = rep_routes * slot_rows + source * CAP + slot_rank
        where_to = jnp.where(kept_pair, where_to, buffer_rows).reshape(-1).astype(jnp.int32)
        kept_flat = kept_pair.reshape(-1)
        owner_slot = jnp.full((buffer_rows,), -1, jnp.int32).at[where_to].set(jnp.arange(rows_rep * TOPK, dtype=jnp.int32), mode="drop")
        valid_row = (owner_slot >= 0)[:, None]
        safe_owner = jnp.maximum(owner_slot, 0)
        token_idx = safe_owner // TOPK
        input_rows = jnp.where(valid_row, rep_tokens[token_idx], jnp.zeros((), jnp.bfloat16)).astype(jnp.bfloat16)
        scaled = (rep_prob[safe_owner][:, None] * rep_grad[token_idx].astype(jnp.float32)).astype(jnp.bfloat16)
        row_gradient = jnp.where(valid_row, scaled, jnp.zeros((), jnp.bfloat16)).astype(jnp.bfloat16)
        results = lax.map(one_expert, (input_rows.reshape(EXPERTS, slot_rows, D), row_gradient.reshape(EXPERTS, slot_rows, D), w_gate, w_up, w_down, up_in, up_out, down_in, down_out))
        slot_gradient = results[0].reshape(buffer_rows, D)
        returned_rows = slot_gradient[jnp.where(kept_flat, where_to, 0)].astype(jnp.float32)
        returned_rows = jnp.where(kept_flat[:, None], returned_rows, jnp.zeros((), jnp.float32))
        pieces.append(jnp.sum(returned_rows.reshape(rows_rep, TOPK, D), axis=1).astype(jnp.bfloat16))
        grad_sums = [grad_sums[index] + results[index + 1] for index in range(4)]
    token_grad = jnp.concatenate(pieces, axis=0)
    return token_grad, grad_sums[0], grad_sums[1], grad_sums[2], grad_sums[3]
```

```python
import jax
import jax.numpy as jnp
from jax import lax
from jax.experimental import pallas as pl
from jax.experimental.pallas import tpu as pltpu
from jax.sharding import PartitionSpec as P

CAP = 3
LANES = 128
COLS = 256
SCALE = 2.0
F32 = jnp.float32
BF16 = jnp.bfloat16

VMEM = pl.BlockSpec(memory_space=pltpu.VMEM)
SMEM = pl.BlockSpec(memory_space=pltpu.SMEM)
ANY = pl.BlockSpec(memory_space=pl.ANY)


def params(mib):
    return pltpu.CompilerParams(vmem_limit_bytes=mib * 1024 * 1024)


def pack_kernel(gate, up, down, packed, sems):
    copies = []
    row = 0
    for ref in (gate, up, down):
        rows, cols = ref.shape[1:]
        for c in range(cols // COLS):
            copies.append(
                pltpu.make_async_copy(
                    ref.at[0, :, pl.ds(c * COLS, COLS)],
                    packed.at[pl.ds(row, rows), :],
                    sems.at[len(copies)],
                )
            )
            row += rows
    for copy in copies:
        copy.start()
    for copy in copies:
        copy.wait()


def pack_weights(w_gate, w_up, w_down):
    size = w_gate.size + w_up.size + w_down.size
    blocks = (w_gate.shape[2] + w_up.shape[2] + w_down.shape[2]) // COLS
    return pl.pallas_call(
        pack_kernel,
        out_shape=jax.ShapeDtypeStruct((size // COLS, COLS), BF16),
        in_specs=[ANY] * 3,
        out_specs=ANY,
        scratch_shapes=[pltpu.SemaphoreType.DMA((blocks,))],
        compiler_params=params(8),
        cost_estimate=pl.CostEstimate(flops=0, bytes_accessed=4 * size, transcendentals=0),
        name="pack_weights",
    )(w_gate, w_up, w_down)


def place_kernel(routes, prob, limits, tokens, grads, send, slots, count):
    experts = send.shape[0]
    send[...] = jnp.zeros_like(send)

    def clear(e, carry):
        count[e] = 0
        return carry

    lax.fori_loop(0, experts, clear, 0)

    def one_token(t, carry):
        row = tokens[t]
        grad = grads[t].astype(F32)
        for k in range(routes.shape[1]):
            e = routes[t, k]
            rank = count[e]
            count[e] = rank + 1
            kept = rank < limits[e]
            slots[t, k] = jnp.where(kept, e * CAP + rank, -1)

            @pl.when(kept)
            def _():
                send[e, rank] = row
                send[e, CAP + rank] = (prob[t, k] * grad).astype(BF16)

        return carry

    lax.fori_loop(0, routes.shape[0], one_token, 0)


def place_rows(routes, prob, limits, tokens, grads):
    count, width = tokens.shape
    subs = width // LANES
    experts = limits.shape[0]
    return pl.pallas_call(
        place_kernel,
        out_shape=(
            jax.ShapeDtypeStruct((experts, 2 * CAP, subs, LANES), BF16),
            jax.ShapeDtypeStruct(routes.shape, jnp.int32),
        ),
        in_specs=[SMEM, SMEM, SMEM, VMEM, VMEM],
        out_specs=(VMEM, SMEM),
        scratch_shapes=[pltpu.SMEM((experts,), jnp.int32)],
        compiler_params=params(16),
        name="place_rows",
    )(routes, prob, limits, tokens.reshape(count, subs, LANES), grads.reshape(count, subs, LANES))


def combine_kernel(slots, back, out):
    def one_token(t, carry):
        total = jnp.zeros(out.shape[1:], F32)
        for k in range(slots.shape[1]):
            slot = slots[t, k]
            row = back[jnp.maximum(slot, 0)].astype(F32)
            total += jnp.where(slot >= 0, row, 0.0)
        out[t] = total.astype(BF16)
        return carry

    lax.fori_loop(0, slots.shape[0], one_token, 0)


def combine_rows(slots, back):
    return pl.pallas_call(
        combine_kernel,
        out_shape=jax.ShapeDtypeStruct((slots.shape[0],) + back.shape[1:], BF16),
        in_specs=[SMEM, VMEM],
        out_specs=VMEM,
        compiler_params=params(16),
        name="combine_rows",
    )(slots, back)


def dot(left, right, left_dim, right_dim):
    return lax.dot_general(
        left, right, (((left_dim,), (right_dim,)), ((), ())), preferred_element_type=F32
    )


def expert_kernel(
    rows_in, rows_grad, packed, up_in, up_out, down_in, down_out,
    slot_grad, adapters,
    gate, up, down, hidden, grad_gate, grad_up, sems,
):
    width, inner = gate.shape
    shards = packed.shape[0]
    part = width // shards
    groups = []
    row = 0
    number = 0
    for ref, by_rows in ((gate, True), (up, True), (down, False)):
        copies = []
        rows, cols = (part, inner) if by_rows else (inner, part)
        for c in range(cols // COLS):
            for s in range(shards):
                if by_rows:
                    target = ref.at[pl.ds(s * part, part), pl.ds(c * COLS, COLS)]
                else:
                    target = ref.at[:, pl.ds(s * part + c * COLS, COLS)]
                copies.append(
                    pltpu.make_async_copy(packed.at[s, pl.ds(row, rows), :], target, sems.at[number])
                )
                number += 1
            row += rows
        groups.append(copies)
    for copies in groups:
        for copy in copies:
            copy.start()

    x = rows_in
    g = rows_grad
    low_up = dot(x[...], up_in[0], 1, 1).astype(BF16)
    back_low = dot(g[...], down_out[0], 1, 1).astype(BF16)
    for copies in groups:
        for copy in copies:
            copy.wait()
    for c in range(inner // COLS):
        cols = pl.ds(c * COLS, COLS)
        gate_pre = dot(x[...], gate[:, cols], 1, 0)
        up_sum = dot(x[...], up[:, cols], 1, 0) + SCALE * dot(low_up, up_out[0, :, cols], 1, 0)
        grad_hidden = dot(g[...], down[cols, :], 1, 1) + SCALE * dot(
            back_low, down_in[0, :, cols], 1, 0
        )
        sig = jax.nn.sigmoid(gate_pre)
        active = gate_pre * sig
        hidden[:, cols] = (active * up_sum).astype(BF16)
        grad_gate[:, cols] = (
            grad_hidden * up_sum * sig * (1.0 + gate_pre * (1.0 - sig))
        ).astype(BF16)
        grad_up[:, cols] = (grad_hidden * active).astype(BF16)
    low_down = dot(hidden[...], down_in[0], 1, 1).astype(BF16)
    up_low = dot(grad_up[...], up_out[0], 1, 1).astype(BF16)
    adapters[:, 0:width] = (SCALE * dot(up_low, x[...], 0, 0)).astype(BF16)
    adapters[:, width : 2 * width] = (SCALE * dot(low_down, g[...], 0, 0)).astype(BF16)
    adapters[:, 2 * width : 2 * width + inner] = (SCALE * dot(low_up, grad_up[...], 0, 0)).astype(BF16)
    adapters[:, 2 * width + inner :] = (SCALE * dot(back_low, hidden[...], 0, 0)).astype(BF16)
    for c in range(width // COLS):
        cols = pl.ds(c * COLS, COLS)
        slot_grad[:, cols] = (
            dot(grad_gate[...], gate[cols, :], 1, 1)
            + dot(grad_up[...], up[cols, :], 1, 1)
            + SCALE * dot(up_low, up_in[0, :, cols], 1, 0)
        ).astype(BF16)


def expert_backward(rows_in, rows_grad, packed, up_in, up_out, down_in, down_out):
    rows, width = rows_in.shape
    rank, inner = up_out.shape[1:]
    return pl.pallas_call(
        expert_kernel,
        out_shape=(
            jax.ShapeDtypeStruct((rows, width), BF16),
            jax.ShapeDtypeStruct((rank, 2 * (width + inner)), BF16),
        ),
        in_specs=[VMEM, VMEM, ANY] + [VMEM] * 4,
        out_specs=(VMEM, VMEM),
        scratch_shapes=[
            pltpu.VMEM((width, inner), BF16),
            pltpu.VMEM((width, inner), BF16),
            pltpu.VMEM((inner, width), BF16),
            pltpu.VMEM((rows, inner), BF16),
            pltpu.VMEM((rows, inner), BF16),
            pltpu.VMEM((rows, inner), BF16),
            pltpu.SemaphoreType.DMA((packed.size // (COLS * (width // packed.shape[0])),)),
        ],
        compiler_params=params(44),
        cost_estimate=pl.CostEstimate(
            flops=10 * rows * width * inner,
            bytes_accessed=6 * width * inner + 6 * rows * width,
            transcendentals=rows * inner,
        ),
        name="expert_backward",
    )(rows_in, rows_grad, packed, up_in, up_out, down_in, down_out)


def on_device(
    tokens, out_grad, gate_prob, routes, limits,
    w_gate, w_up, w_down, up_in, up_out, down_in, down_out,
):
    width = tokens.shape[1]
    inner = up_out.shape[2]
    experts = limits.shape[0]
    slot_rows = experts * CAP
    packed = lax.all_gather(pack_weights(w_gate, w_up, w_down), "rep")
    send, slots = place_rows(routes, gate_prob, limits, tokens, out_grad)
    recv = lax.all_to_all(send, ("grp", "exp"), split_axis=0, concat_axis=0, tiled=True)
    rows_in = recv[:, :CAP].reshape(slot_rows, width)
    rows_grad = recv[:, CAP:].reshape(slot_rows, width)
    slot_grad, adapters = expert_backward(
        rows_in, rows_grad, packed, up_in, up_out, down_in, down_out
    )
    adapters = lax.psum(adapters, "rep").astype(F32)
    back = lax.all_to_all(
        slot_grad.reshape(experts, CAP, width // LANES, LANES),
        ("grp", "exp"), split_axis=0, concat_axis=0, tiled=True,
    )
    token_grad = combine_rows(slots, back.reshape(slot_rows, width // LANES, LANES))
    return (
        token_grad.reshape(tokens.shape),
        adapters[None, :, 0:width],
        adapters[None, :, 2 * width : 2 * width + inner],
        adapters[None, :, 2 * width + inner :],
        adapters[None, :, width : 2 * width],
    )


def solution(mesh):
    rows = P(("rep", "grp", "exp"), None)
    owner = P(("grp", "exp"), None, None)
    return jax.shard_map(
        on_device,
        mesh=mesh,
        in_specs=(
            rows, rows, rows, rows, P(),
            P(("grp", "exp"), "rep", None),
            P(("grp", "exp"), "rep", None),
            P(("grp", "exp"), None, "rep"),
            owner, owner, owner, owner,
        ),
        out_specs=(rows, owner, owner, owner, owner),
        check_vma=False,
    )
```

```python
import jax
import jax.numpy as jnp
from jax import lax
from jax.experimental import pallas as pl
from jax.experimental.pallas import tpu as pltpu
from jax.sharding import PartitionSpec as P

CAP = 3
LANES = 128
COLS = 256
SCALE = 2.0
F32 = jnp.float32
BF16 = jnp.bfloat16

VMEM = pl.BlockSpec(memory_space=pltpu.VMEM)
SMEM = pl.BlockSpec(memory_space=pltpu.SMEM)
ANY = pl.BlockSpec(memory_space=pl.ANY)


def params(mib):
    return pltpu.CompilerParams(vmem_limit_bytes=mib * 1024 * 1024)


def pack_kernel(gate, up, down, packed, sems):
    copies = []
    row = 0
    for ref in (gate, up, down):
        rows, cols = ref.shape[1:]
        for c in range(cols // COLS):
            copies.append(
                pltpu.make_async_copy(
                    ref.at[0, :, pl.ds(c * COLS, COLS)],
                    packed.at[pl.ds(row, rows), :],
                    sems.at[len(copies)],
                )
            )
            row += rows
    for copy in copies:
        copy.start()
    for copy in copies:
        copy.wait()


def pack_weights(w_gate, w_up, w_down):
    size = w_gate.size + w_up.size + w_down.size
    blocks = (w_gate.shape[2] + w_up.shape[2] + w_down.shape[2]) // COLS
    return pl.pallas_call(
        pack_kernel,
        out_shape=jax.ShapeDtypeStruct((size // COLS, COLS), BF16),
        in_specs=[ANY] * 3,
        out_specs=ANY,
        scratch_shapes=[pltpu.SemaphoreType.DMA((blocks,))],
        compiler_params=params(56),
        cost_estimate=pl.CostEstimate(flops=0, bytes_accessed=4 * size, transcendentals=0),
        name="pack_weights",
    )(w_gate, w_up, w_down)


def place_kernel(routes, prob, limits, tokens, grads, send, slots, count, staged):
    total = send.shape[0]
    staged[...] = jnp.zeros_like(staged)

    def clear(e, carry):
        count[e] = 0
        return carry

    lax.fori_loop(0, limits.shape[0], clear, 0, unroll=8)

    def one_token(t, carry):
        row = tokens[t]
        grad = grads[t].astype(F32)
        for k in range(routes.shape[1]):
            e = routes[t, k]
            rank = count[e]
            count[e] = rank + 1
            kept = rank < limits[e]
            slots[t, k] = jnp.where(kept, e * CAP + rank, -1)
            place = jnp.where(kept, e * (2 * CAP) + rank, total)
            staged[place] = row
            staged[place + CAP] = (prob[t, k] * grad).astype(BF16)
        return carry

    lax.fori_loop(0, routes.shape[0], one_token, 0)
    send[...] = staged[0:total]


def place_rows(routes, prob, limits, tokens, grads):
    count, width = tokens.shape
    subs = width // LANES
    experts = limits.shape[0]
    total = experts * 2 * CAP
    return pl.pallas_call(
        place_kernel,
        out_shape=(
            jax.ShapeDtypeStruct((total, subs, LANES), BF16),
            jax.ShapeDtypeStruct(routes.shape, jnp.int32),
        ),
        in_specs=[SMEM, SMEM, SMEM, VMEM, VMEM],
        out_specs=(VMEM, SMEM),
        scratch_shapes=[
            pltpu.SMEM((experts,), jnp.int32),
            pltpu.VMEM((total + 2 * CAP, subs, LANES), BF16),
        ],
        compiler_params=params(16),
        name="place_rows",
    )(routes, prob, limits, tokens.reshape(count, subs, LANES), grads.reshape(count, subs, LANES))


def combine_kernel(slots, back, out):
    def one_token(t, carry):
        total = jnp.zeros(out.shape[1:], F32)
        for k in range(slots.shape[1]):
            slot = slots[t, k]
            row = back[jnp.maximum(slot, 0)].astype(F32)
            total += jnp.where(slot >= 0, row, 0.0)
        out[t] = total.astype(BF16)
        return carry

    lax.fori_loop(0, slots.shape[0], one_token, 0)


def combine_rows(slots, back):
    return pl.pallas_call(
        combine_kernel,
        out_shape=jax.ShapeDtypeStruct((slots.shape[0],) + back.shape[1:], BF16),
        in_specs=[SMEM, VMEM],
        out_specs=VMEM,
        compiler_params=params(16),
        name="combine_rows",
    )(slots, back)


def dot(left, right, left_dim, right_dim):
    return lax.dot_general(
        left, right, (((left_dim,), (right_dim,)), ((), ())), preferred_element_type=F32
    )


def slot_kernel(
    rows_in, rows_grad, packed, up_in, up_out, down_in, down_out,
    slot_grad, hidden, grad_up, low_up, back_low, up_low,
    gate, up, down, grad_gate, sems,
):
    width, inner = gate.shape
    shards = packed.shape[0]
    part = width // shards
    chunks = inner // COLS
    steps = []
    number = 0
    for c in range(chunks):
        cols = pl.ds(c * COLS, COLS)
        moves = []
        for s in range(shards):
            for base, ref in ((0, gate), (chunks * part, up)):
                moves.append(
                    (packed.at[s, pl.ds(base + c * part, part), :], ref.at[pl.ds(s * part, part), cols])
                )
        for s in range(shards):
            for m in range(part // COLS):
                row = 2 * chunks * part + m * inner + c * COLS
                moves.append(
                    (packed.at[s, pl.ds(row, COLS), :], down.at[cols, pl.ds(s * part + m * COLS, COLS)])
                )
        copies = []
        for source, target in moves:
            copies.append(pltpu.make_async_copy(source, target, sems.at[number]))
            number += 1
        steps.append(copies)
    for copies in steps:
        for copy in copies:
            copy.start()

    x = rows_in
    g = rows_grad
    low_up[...] = dot(x[...], up_in[0], 1, 1).astype(BF16)
    back_low[...] = dot(g[...], down_out[0], 1, 1).astype(BF16)
    for c in range(chunks):
        cols = pl.ds(c * COLS, COLS)
        for copy in steps[c]:
            copy.wait()
        gate_pre = dot(x[...], gate[:, cols], 1, 0)
        up_sum = dot(x[...], up[:, cols], 1, 0) + SCALE * dot(low_up[...], up_out[0, :, cols], 1, 0)
        grad_hidden = dot(g[...], down[cols, :], 1, 1) + SCALE * dot(
            back_low[...], down_in[0, :, cols], 1, 0
        )
        sig = jax.nn.sigmoid(gate_pre)
        active = gate_pre * sig
        hidden[:, cols] = (active * up_sum).astype(BF16)
        grad_gate[:, cols] = (
            grad_hidden * up_sum * sig * (1.0 + gate_pre * (1.0 - sig))
        ).astype(BF16)
        grad_up[:, cols] = (grad_hidden * active).astype(BF16)
    up_low[...] = dot(grad_up[...], up_out[0], 1, 1).astype(BF16)
    for c in range(width // COLS):
        cols = pl.ds(c * COLS, COLS)
        slot_grad[:, cols] = (
            dot(grad_gate[...], gate[cols, :], 1, 1)
            + dot(grad_up[...], up[cols, :], 1, 1)
            + SCALE * dot(up_low[...], up_in[0, :, cols], 1, 0)
        ).astype(BF16)


def adapter_kernel(rows_in, rows_grad, hidden, grad_up, low_up, back_low, up_low, down_in, adapters):
    width, inner = rows_in.shape[1], hidden.shape[1]
    low_down = dot(hidden[...], down_in[0], 1, 1).astype(BF16)
    at = 0
    for left, right in (
        (up_low[...], rows_in),
        (low_down, rows_grad),
        (low_up[...], grad_up),
        (back_low[...], hidden),
    ):
        for c in range(right.shape[1] // COLS):
            piece = dot(left, right[:, pl.ds(c * COLS, COLS)], 0, 0)
            adapters[:, pl.ds(at, COLS)] = (SCALE * piece).astype(BF16)
            at += COLS


def expert_slots(rows_in, rows_grad, packed, up_in, up_out, down_in, down_out):
    rows, width = rows_in.shape
    rank, inner = up_out.shape[1:]
    shards = packed.shape[0]
    part = width // shards
    return pl.pallas_call(
        slot_kernel,
        out_shape=(
            jax.ShapeDtypeStruct((rows, width), BF16),
            jax.ShapeDtypeStruct((rows, inner), BF16),
            jax.ShapeDtypeStruct((rows, inner), BF16),
            jax.ShapeDtypeStruct((rows, rank), BF16),
            jax.ShapeDtypeStruct((rows, rank), BF16),
            jax.ShapeDtypeStruct((rows, rank), BF16),
        ),
        in_specs=[VMEM, VMEM, ANY] + [VMEM] * 4,
        out_specs=(VMEM,) * 6,
        scratch_shapes=[
            pltpu.VMEM((width, inner), BF16),
            pltpu.VMEM((width, inner), BF16),
            pltpu.VMEM((inner, width), BF16),
            pltpu.VMEM((rows, inner), BF16),
            pltpu.SemaphoreType.DMA((shards * (2 + part // COLS) * (inner // COLS),)),
        ],
        compiler_params=params(44),
        cost_estimate=pl.CostEstimate(
            flops=10 * rows * width * inner,
            bytes_accessed=6 * width * inner + 6 * rows * width,
            transcendentals=rows * inner,
        ),
        name="expert_slots",
    )(rows_in, rows_grad, packed, up_in, up_out, down_in, down_out)


def adapter_grads(rows_in, rows_grad, hidden, grad_up, low_up, back_low, up_low, down_in):
    rows, width = rows_in.shape
    inner = hidden.shape[1]
    rank = up_low.shape[1]
    return pl.pallas_call(
        adapter_kernel,
        out_shape=jax.ShapeDtypeStruct((rank, 2 * (width + inner)), BF16),
        in_specs=[VMEM] * 8,
        out_specs=VMEM,
        compiler_params=params(24),
        cost_estimate=pl.CostEstimate(
            flops=4 * rows * rank * (width + inner),
            bytes_accessed=4 * rows * (width + inner),
            transcendentals=0,
        ),
        name="adapter_grads",
    )(rows_in, rows_grad, hidden, grad_up, low_up, back_low, up_low, down_in)


def replica_sum(own, axis):
    count = lax.axis_size(axis)
    total = own.astype(F32)
    for shift in range(1, count):
        pairs = [(i, (i + shift) % count) for i in range(count)]
        total += lax.ppermute(own, axis, pairs).astype(F32)
    return total


def on_device(
    tokens, out_grad, gate_prob, routes, limits,
    w_gate, w_up, w_down, up_in, up_out, down_in, down_out,
):
    width = tokens.shape[1]
    inner = up_out.shape[2]
    experts = limits.shape[0]
    slot_rows = experts * CAP
    packed = lax.all_gather(pack_weights(w_gate, w_up, w_down), "rep")
    send, slots = place_rows(routes, gate_prob, limits, tokens, out_grad)
    send = send.reshape(experts, 2 * CAP, width // LANES, LANES)
    recv = lax.all_to_all(send, ("grp", "exp"), split_axis=0, concat_axis=0, tiled=True)
    rows_in = recv[:, :CAP].reshape(slot_rows, width)
    rows_grad = recv[:, CAP:].reshape(slot_rows, width)
    slot_grad, *kept = expert_slots(rows_in, rows_grad, packed, up_in, up_out, down_in, down_out)
    adapters = replica_sum(adapter_grads(rows_in, rows_grad, *kept, down_in), "rep")
    back = lax.all_to_all(
        slot_grad.reshape(experts, CAP, width // LANES, LANES),
        ("grp", "exp"), split_axis=0, concat_axis=0, tiled=True,
    )
    token_grad = combine_rows(slots, back.reshape(slot_rows, width // LANES, LANES))
    return (
        token_grad.reshape(tokens.shape),
        adapters[None, :, 0:width],
        adapters[None, :, 2 * width : 2 * width + inner],
        adapters[None, :, 2 * width + inner :],
        adapters[None, :, width : 2 * width],
    )


def solution(mesh):
    rows = P(("rep", "grp", "exp"), None)
    owner = P(("grp", "exp"), None, None)
    return jax.shard_map(
        on_device,
        mesh=mesh,
        in_specs=(
            rows, rows, rows, rows, P(),
            P(("grp", "exp"), "rep", None),
            P(("grp", "exp"), "rep", None),
            P(("grp", "exp"), None, "rep"),
            owner, owner, owner, owner,
        ),
        out_specs=(rows, owner, owner, owner, owner),
        check_vma=False,
    )
```

```python
import jax
import jax.numpy as jnp
from jax import lax
from jax.experimental import pallas as pl
from jax.experimental.pallas import tpu as pltpu
from jax.sharding import PartitionSpec as P

CAP = 3
LANES = 128
COLS = 256
SCALE = 2.0
F32 = jnp.float32
BF16 = jnp.bfloat16

VMEM = pl.BlockSpec(memory_space=pltpu.VMEM)
SMEM = pl.BlockSpec(memory_space=pltpu.SMEM)
HBM = pl.BlockSpec(memory_space=pltpu.HBM)


def params(mib):
    return pltpu.CompilerParams(vmem_limit_bytes=mib * 1024 * 1024)


def pack_kernel(gate, up, packed, staged, sems):
    moves = []
    row = 0
    for ref in (gate, up):
        rows, cols = ref.shape[1:]
        for c in range(cols // COLS):
            place = pl.ds(row, rows)
            i = len(moves)
            moves.append(
                (
                    pltpu.make_async_copy(ref.at[0, :, pl.ds(c * COLS, COLS)], staged.at[place, :], sems.at[0, i]),
                    pltpu.make_async_copy(staged.at[place, :], packed.at[place, :], sems.at[1, i]),
                )
            )
            row += rows
    for load, _ in moves:
        load.start()
    for load, store in moves:
        load.wait()
        store.start()
    for _, store in moves:
        store.wait()


def pack_weights(w_gate, w_up):
    size = w_gate.size + w_up.size
    blocks = (w_gate.shape[2] + w_up.shape[2]) // COLS
    return pl.pallas_call(
        pack_kernel,
        out_shape=jax.ShapeDtypeStruct((size // COLS, COLS), BF16),
        in_specs=[HBM] * 2,
        out_specs=HBM,
        scratch_shapes=[
            pltpu.VMEM((size // COLS, COLS), BF16),
            pltpu.SemaphoreType.DMA((2, blocks)),
        ],
        compiler_params=params(56),
        cost_estimate=pl.CostEstimate(flops=0, bytes_accessed=4 * size, transcendentals=0),
        name="pack_weights",
    )(w_gate, w_up)


def place_kernel(routes, prob, limits, tokens, grads, send, slots, count, staged):
    total = send.shape[0]
    staged[...] = jnp.zeros_like(staged)

    def clear(e, carry):
        count[e] = 0
        return carry

    lax.fori_loop(0, limits.shape[0], clear, 0, unroll=8)

    def one_token(t, carry):
        row = tokens[t]
        grad = grads[t].astype(F32)
        for k in range(routes.shape[1]):
            e = routes[t, k]
            rank = count[e]
            count[e] = rank + 1
            kept = rank < limits[e]
            slots[t, k] = jnp.where(kept, e * CAP + rank, -1)
            place = jnp.where(kept, e * (2 * CAP) + rank, total)
            staged[place] = row
            staged[place + CAP] = (prob[t, k] * grad).astype(BF16)
        return carry

    lax.fori_loop(0, routes.shape[0], one_token, 0)
    send[...] = staged[0:total]


def place_rows(routes, prob, limits, tokens, grads):
    count, width = tokens.shape
    subs = width // LANES
    experts = limits.shape[0]
    total = experts * 2 * CAP
    return pl.pallas_call(
        place_kernel,
        out_shape=(
            jax.ShapeDtypeStruct((total, subs, LANES), BF16),
            jax.ShapeDtypeStruct(routes.shape, jnp.int32),
        ),
        in_specs=[SMEM, SMEM, SMEM, VMEM, VMEM],
        out_specs=(VMEM, SMEM),
        scratch_shapes=[
            pltpu.SMEM((experts,), jnp.int32),
            pltpu.VMEM((total + 2 * CAP, subs, LANES), BF16),
        ],
        compiler_params=params(16),
        name="place_rows",
    )(routes, prob, limits, tokens.reshape(count, subs, LANES), grads.reshape(count, subs, LANES))


def combine_kernel(slots, back, out):
    def one_token(t, carry):
        total = jnp.zeros(out.shape[1:], F32)
        for k in range(slots.shape[1]):
            slot = slots[t, k]
            row = back[jnp.maximum(slot, 0)].astype(F32)
            total += jnp.where(slot >= 0, row, 0.0)
        out[t] = total.astype(BF16)
        return carry

    lax.fori_loop(0, slots.shape[0], one_token, 0)


def combine_rows(slots, back):
    return pl.pallas_call(
        combine_kernel,
        out_shape=jax.ShapeDtypeStruct((slots.shape[0],) + back.shape[1:], BF16),
        in_specs=[SMEM, VMEM],
        out_specs=VMEM,
        compiler_params=params(16),
        name="combine_rows",
    )(slots, back)


def dot(left, right, left_dim, right_dim):
    return lax.dot_general(
        left, right, (((left_dim,), (right_dim,)), ((), ())), preferred_element_type=F32
    )


def slot_kernel(
    mine, rows_in, rows_grad, packed, down_0, down_1, down_2, down_3,
    up_in_far, up_out_far, down_in_far, down_out_far,
    slot_grad, hidden, grad_up, low_up, back_low, up_low,
    gate, up, down, grad_gate, up_in, up_out, down_in, down_out, sems,
):
    width, inner = gate.shape
    shards = packed.shape[0]
    part = width // shards
    chunks = inner // COLS
    steps = []
    small = []
    number = 0
    for source, target in ((up_in_far, up_in), (down_out_far, down_out), (up_out_far, up_out), (down_in_far, down_in)):
        small.append(pltpu.make_async_copy(source, target, sems.at[number]))
        number += 1
    for c in range(chunks):
        cols = pl.ds(c * COLS, COLS)
        moves = []
        for s in range(shards):
            for base, ref in ((0, gate), (chunks * part, up)):
                moves.append(
                    (packed.at[s, pl.ds(base + c * part, part), :], ref.at[pl.ds(s * part, part), cols])
                )
        for s, ref in enumerate((down_0, down_1, down_2, down_3)):
            owner = lax.rem(mine[0] + (shards - s), shards)
            place = pl.multiple_of(owner * part, part)
            moves.append((ref.at[0, cols, :], down.at[cols, pl.ds(place, part)]))
        copies = []
        for source, target in moves:
            copies.append(pltpu.make_async_copy(source, target, sems.at[number]))
            number += 1
        steps.append(copies)
    for copies in [small] + steps:
        for copy in copies:
            copy.start()

    x = rows_in
    g = rows_grad
    for copy in small:
        copy.wait()
    low_up[...] = dot(x[...], up_in[0], 1, 1).astype(BF16)
    back_low[...] = dot(g[...], down_out[0], 1, 1).astype(BF16)
    for c in range(chunks):
        cols = pl.ds(c * COLS, COLS)
        for copy in steps[c]:
            copy.wait()
        gate_pre = dot(x[...], gate[:, cols], 1, 0)
        up_sum = dot(x[...], up[:, cols], 1, 0) + SCALE * dot(low_up[...], up_out[0, :, cols], 1, 0)
        grad_hidden = dot(g[...], down[cols, :], 1, 1) + SCALE * dot(
            back_low[...], down_in[0, :, cols], 1, 0
        )
        sig = jax.nn.sigmoid(gate_pre)
        active = gate_pre * sig
        hidden[:, cols] = (active * up_sum).astype(BF16)
        grad_gate[:, cols] = (
            grad_hidden * up_sum * sig * (1.0 + gate_pre * (1.0 - sig))
        ).astype(BF16)
        grad_up[:, cols] = (grad_hidden * active).astype(BF16)
    up_low[...] = dot(grad_up[...], up_out[0], 1, 1).astype(BF16)
    for c in range(width // COLS):
        cols = pl.ds(c * COLS, COLS)
        slot_grad[:, cols] = (
            dot(grad_gate[...], gate[cols, :], 1, 1)
            + dot(grad_up[...], up[cols, :], 1, 1)
            + SCALE * dot(up_low[...], up_in[0, :, cols], 1, 0)
        ).astype(BF16)


def adapter_kernel(rows_in, rows_grad, hidden, grad_up, low_up, back_low, up_low, down_in, adapters):
    width, inner = rows_in.shape[1], hidden.shape[1]
    low_down = dot(hidden[...], down_in[0], 1, 1).astype(BF16)
    at = 0
    for left, right in (
        (up_low[...], rows_in),
        (low_down, rows_grad),
        (low_up[...], grad_up),
        (back_low[...], hidden),
    ):
        for c in range(right.shape[1] // COLS):
            piece = dot(left, right[:, pl.ds(c * COLS, COLS)], 0, 0)
            adapters[:, pl.ds(at, COLS)] = (SCALE * piece).astype(BF16)
            at += COLS


def expert_slots(mine, rows_in, rows_grad, packed, downs, up_in, up_out, down_in, down_out):
    rows, width = rows_in.shape
    rank, inner = up_out.shape[1:]
    shards = packed.shape[0]
    part = width // shards
    return pl.pallas_call(
        slot_kernel,
        out_shape=(
            jax.ShapeDtypeStruct((rows, width), BF16),
            jax.ShapeDtypeStruct((rows, inner), BF16),
            jax.ShapeDtypeStruct((rows, inner), BF16),
            jax.ShapeDtypeStruct((rows, rank), BF16),
            jax.ShapeDtypeStruct((rows, rank), BF16),
            jax.ShapeDtypeStruct((rows, rank), BF16),
        ),
        in_specs=[SMEM, VMEM, VMEM] + [HBM] * 9,
        out_specs=(VMEM,) * 6,
        scratch_shapes=[
            pltpu.VMEM((width, inner), BF16),
            pltpu.VMEM((width, inner), BF16),
            pltpu.VMEM((inner, width), BF16),
            pltpu.VMEM((rows, inner), BF16),
            pltpu.VMEM((1, rank, width), BF16),
            pltpu.VMEM((1, rank, inner), BF16),
            pltpu.VMEM((1, rank, inner), BF16),
            pltpu.VMEM((1, rank, width), BF16),
            pltpu.SemaphoreType.DMA((4 + 3 * shards * (inner // COLS),)),
        ],
        compiler_params=params(54),
        cost_estimate=pl.CostEstimate(
            flops=10 * rows * width * inner,
            bytes_accessed=6 * width * inner + 6 * rows * width,
            transcendentals=rows * inner,
        ),
        name="expert_slots",
    )(mine, rows_in, rows_grad, packed, *downs, up_in, up_out, down_in, down_out)


def adapter_grads(rows_in, rows_grad, hidden, grad_up, low_up, back_low, up_low, down_in):
    rows, width = rows_in.shape
    inner = hidden.shape[1]
    rank = up_low.shape[1]
    return pl.pallas_call(
        adapter_kernel,
        out_shape=jax.ShapeDtypeStruct((rank, 2 * (width + inner)), BF16),
        in_specs=[VMEM] * 8,
        out_specs=VMEM,
        compiler_params=params(24),
        cost_estimate=pl.CostEstimate(
            flops=4 * rows * rank * (width + inner),
            bytes_accessed=4 * rows * (width + inner),
            transcendentals=0,
        ),
        name="adapter_grads",
    )(rows_in, rows_grad, hidden, grad_up, low_up, back_low, up_low, down_in)


def messages(own, axis):
    count = lax.axis_size(axis)
    return [
        lax.ppermute(own, axis, [(i, (i + shift) % count) for i in range(count)])
        for shift in range(1, count)
    ]


def replica_sum(own, axis):
    total = own.astype(F32)
    for other in messages(own, axis):
        total += other.astype(F32)
    return total


def on_device(
    tokens, out_grad, gate_prob, routes, limits,
    w_gate, w_up, w_down, up_in, up_out, down_in, down_out,
):
    width = tokens.shape[1]
    inner = up_out.shape[2]
    experts = limits.shape[0]
    slot_rows = experts * CAP
    packed = lax.all_gather(pack_weights(w_gate, w_up), "rep")
    downs = [w_down] + messages(w_down, "rep")
    send, slots = place_rows(routes, gate_prob, limits, tokens, out_grad)
    send = send.reshape(experts, 2 * CAP, width // LANES, LANES)
    recv = lax.all_to_all(send, ("grp", "exp"), split_axis=0, concat_axis=0, tiled=True)
    rows_in = recv[:, :CAP].reshape(slot_rows, width)
    rows_grad = recv[:, CAP:].reshape(slot_rows, width)
    mine = lax.axis_index("rep").astype(jnp.int32).reshape(1)
    slot_grad, *kept = expert_slots(mine, rows_in, rows_grad, packed, downs, up_in, up_out, down_in, down_out)
    adapters = replica_sum(adapter_grads(rows_in, rows_grad, *kept, down_in), "rep")
    back = lax.all_to_all(
        slot_grad.reshape(experts, CAP, width // LANES, LANES),
        ("grp", "exp"), split_axis=0, concat_axis=0, tiled=True,
    )
    token_grad = combine_rows(slots, back.reshape(slot_rows, width // LANES, LANES))
    return (
        token_grad.reshape(tokens.shape),
        adapters[None, :, 0:width],
        adapters[None, :, 2 * width : 2 * width + inner],
        adapters[None, :, 2 * width + inner :],
        adapters[None, :, width : 2 * width],
    )


def solution(mesh):
    rows = P(("rep", "grp", "exp"), None)
    owner = P(("grp", "exp"), None, None)
    return jax.shard_map(
        on_device,
        mesh=mesh,
        in_specs=(
            rows, rows, rows, rows, P(),
            P(("grp", "exp"), "rep", None),
            P(("grp", "exp"), "rep", None),
            P(("grp", "exp"), None, "rep"),
            owner, owner, owner, owner,
        ),
        out_specs=(rows, owner, owner, owner, owner),
        check_vma=False,
    )
```

```python
import jax
import jax.numpy as jnp
from jax import lax
from jax.experimental import pallas as pl
from jax.experimental.pallas import tpu as pltpu
from jax.sharding import PartitionSpec as P

CAP = 3
LANES = 128
COLS = 256
SCALE = 2.0
F32 = jnp.float32
BF16 = jnp.bfloat16

VMEM = pl.BlockSpec(memory_space=pltpu.VMEM)
SMEM = pl.BlockSpec(memory_space=pltpu.SMEM)
HBM = pl.BlockSpec(memory_space=pltpu.HBM)


def params(mib):
    return pltpu.CompilerParams(vmem_limit_bytes=mib * 1024 * 1024)


def pack_kernel(gate, up, down, packed, staged, sems):
    moves = []
    row = 0
    for ref in (gate, up, down):
        rows, cols = ref.shape[1:]
        for c in range(cols // COLS):
            place = pl.ds(row, rows)
            i = len(moves)
            moves.append(
                (
                    pltpu.make_async_copy(ref.at[0, :, pl.ds(c * COLS, COLS)], staged.at[place, :], sems.at[0, i]),
                    pltpu.make_async_copy(staged.at[place, :], packed.at[place, :], sems.at[1, i]),
                )
            )
            row += rows
    for load, _ in moves:
        load.start()
    for load, store in moves:
        load.wait()
        store.start()
    for _, store in moves:
        store.wait()


def pack_weights(w_gate, w_up, w_down):
    size = w_gate.size + w_up.size + w_down.size
    blocks = (w_gate.shape[2] + w_up.shape[2] + w_down.shape[2]) // COLS
    return pl.pallas_call(
        pack_kernel,
        out_shape=jax.ShapeDtypeStruct((size // COLS, COLS), BF16),
        in_specs=[HBM] * 3,
        out_specs=HBM,
        scratch_shapes=[
            pltpu.VMEM((size // COLS, COLS), BF16),
            pltpu.SemaphoreType.DMA((2, blocks)),
        ],
        compiler_params=params(56),
        cost_estimate=pl.CostEstimate(flops=0, bytes_accessed=4 * size, transcendentals=0),
        name="pack_weights",
    )(w_gate, w_up, w_down)


def place_kernel(routes, prob, limits, tokens, grads, send, slots, count, staged):
    total = send.shape[0]
    staged[...] = jnp.zeros_like(staged)

    def clear(e, carry):
        count[e] = 0
        return carry

    lax.fori_loop(0, limits.shape[0], clear, 0, unroll=8)

    def one_token(t, carry):
        row = tokens[t]
        grad = grads[t].astype(F32)
        for k in range(routes.shape[1]):
            e = routes[t, k]
            rank = count[e]
            count[e] = rank + 1
            kept = rank < limits[e]
            slots[t, k] = jnp.where(kept, e * CAP + rank, -1)
            place = jnp.where(kept, e * (2 * CAP) + rank, total)
            staged[place] = row
            staged[place + CAP] = (prob[t, k] * grad).astype(BF16)
        return carry

    lax.fori_loop(0, routes.shape[0], one_token, 0)
    send[...] = staged[0:total]


def place_rows(routes, prob, limits, tokens, grads):
    count, width = tokens.shape
    subs = width // LANES
    experts = limits.shape[0]
    total = experts * 2 * CAP
    return pl.pallas_call(
        place_kernel,
        out_shape=(
            jax.ShapeDtypeStruct((total, subs, LANES), BF16),
            jax.ShapeDtypeStruct(routes.shape, jnp.int32),
        ),
        in_specs=[SMEM, SMEM, SMEM, VMEM, VMEM],
        out_specs=(VMEM, SMEM),
        scratch_shapes=[
            pltpu.SMEM((experts,), jnp.int32),
            pltpu.VMEM((total + 2 * CAP, subs, LANES), BF16),
        ],
        compiler_params=params(16),
        name="place_rows",
    )(routes, prob, limits, tokens.reshape(count, subs, LANES), grads.reshape(count, subs, LANES))


def combine_kernel(slots, back, out):
    def one_token(t, carry):
        total = jnp.zeros(out.shape[1:], F32)
        for k in range(slots.shape[1]):
            slot = slots[t, k]
            row = back[jnp.maximum(slot, 0)].astype(F32)
            total += jnp.where(slot >= 0, row, 0.0)
        out[t] = total.astype(BF16)
        return carry

    lax.fori_loop(0, slots.shape[0], one_token, 0)


def combine_rows(slots, back):
    return pl.pallas_call(
        combine_kernel,
        out_shape=jax.ShapeDtypeStruct((slots.shape[0],) + back.shape[1:], BF16),
        in_specs=[SMEM, VMEM],
        out_specs=VMEM,
        compiler_params=params(16),
        name="combine_rows",
    )(slots, back)


def dot(left, right, left_dim, right_dim):
    return lax.dot_general(
        left, right, (((left_dim,), (right_dim,)), ((), ())), preferred_element_type=F32
    )


def low_kernel(rows_in, rows_grad, up_in, down_out, low_up, back_low, up_in_near):
    low_up[...] = dot(rows_in[...], up_in[0], 1, 1).astype(BF16)
    back_low[...] = dot(rows_grad[...], down_out[0], 1, 1).astype(BF16)
    up_in_near[...] = up_in[0]


def low_products(rows_in, rows_grad, up_in, down_out):
    rows, width = rows_in.shape
    rank = up_in.shape[1]
    return pl.pallas_call(
        low_kernel,
        out_shape=(
            jax.ShapeDtypeStruct((rows, rank), BF16),
            jax.ShapeDtypeStruct((rows, rank), BF16),
            jax.ShapeDtypeStruct((rank, width), BF16),
        ),
        in_specs=[VMEM] * 4,
        out_specs=(VMEM,) * 3,
        compiler_params=params(16),
        cost_estimate=pl.CostEstimate(
            flops=4 * rows * rank * width, bytes_accessed=4 * rows * width, transcendentals=0
        ),
        name="low_products",
    )(rows_in, rows_grad, up_in, down_out)


def slot_kernel(
    rows_in, rows_grad, packed, low_up, back_low, up_in, up_out, down_in,
    slot_grad, hidden, grad_up, up_low,
    gate_up, down, grads, sems,
):
    width = gate_up.shape[0]
    inner = hidden.shape[1]
    shards = packed.shape[0]
    part = width // shards
    chunks = inner // COLS
    steps = []
    number = 0
    for c in range(chunks):
        cols = pl.ds(c * COLS, COLS)
        moves = []
        for s in range(shards):
            for i in range(2):
                moves.append(
                    (
                        packed.at[s, pl.ds((i * chunks + c) * part, part), :],
                        gate_up.at[pl.ds(s * part, part), pl.ds(i * inner + c * COLS, COLS)],
                    )
                )
        for s in range(shards):
            for m in range(part // COLS):
                row = 2 * chunks * part + m * inner + c * COLS
                moves.append(
                    (packed.at[s, pl.ds(row, COLS), :], down.at[cols, pl.ds(s * part + m * COLS, COLS)])
                )
        copies = []
        for source, target in moves:
            copies.append(pltpu.make_async_copy(source, target, sems.at[number]))
            number += 1
        steps.append(copies)
    for copies in steps:
        for copy in copies:
            copy.start()

    x = rows_in
    g = rows_grad
    for c in range(chunks):
        cols = pl.ds(c * COLS, COLS)
        later = pl.ds(inner + c * COLS, COLS)
        for copy in steps[c]:
            copy.wait()
        gate_pre = dot(x[...], gate_up[:, cols], 1, 0)
        up_sum = dot(x[...], gate_up[:, later], 1, 0) + SCALE * dot(low_up[...], up_out[0, :, cols], 1, 0)
        grad_hidden = dot(g[...], down[cols, :], 1, 1) + SCALE * dot(
            back_low[...], down_in[0, :, cols], 1, 0
        )
        sig = jax.nn.sigmoid(gate_pre)
        active = gate_pre * sig
        up_grad = (grad_hidden * active).astype(BF16)
        hidden[:, cols] = (active * up_sum).astype(BF16)
        grads[:, cols] = (
            grad_hidden * up_sum * sig * (1.0 + gate_pre * (1.0 - sig))
        ).astype(BF16)
        grads[:, later] = up_grad
        grad_up[:, cols] = up_grad
    up_low[...] = dot(grad_up[...], up_out[0], 1, 1).astype(BF16)
    for c in range(width // COLS):
        cols = pl.ds(c * COLS, COLS)
        slot_grad[:, cols] = (
            dot(grads[...], gate_up[cols, :], 1, 1) + SCALE * dot(up_low[...], up_in[:, cols], 1, 0)
        ).astype(BF16)


def adapter_kernel(rows_in, rows_grad, hidden, grad_up, low_up, back_low, up_low, down_in, adapters):
    width, inner = rows_in.shape[1], hidden.shape[1]
    low_down = dot(hidden[...], down_in[0], 1, 1).astype(BF16)
    at = 0
    for left, right in (
        (up_low[...], rows_in),
        (low_down, rows_grad),
        (low_up[...], grad_up),
        (back_low[...], hidden),
    ):
        for c in range(right.shape[1] // COLS):
            piece = dot(left, right[:, pl.ds(c * COLS, COLS)], 0, 0)
            adapters[:, pl.ds(at, COLS)] = (SCALE * piece).astype(BF16)
            at += COLS


def expert_slots(rows_in, rows_grad, packed, low_up, back_low, up_in, up_out, down_in):
    rows, width = rows_in.shape
    rank, inner = up_out.shape[1:]
    shards = packed.shape[0]
    part = width // shards
    return pl.pallas_call(
        slot_kernel,
        out_shape=(
            jax.ShapeDtypeStruct((rows, width), BF16),
            jax.ShapeDtypeStruct((rows, inner), BF16),
            jax.ShapeDtypeStruct((rows, inner), BF16),
            jax.ShapeDtypeStruct((rows, rank), BF16),
        ),
        in_specs=[VMEM, VMEM, HBM] + [VMEM] * 5,
        out_specs=(VMEM,) * 4,
        scratch_shapes=[
            pltpu.VMEM((width, 2 * inner), BF16),
            pltpu.VMEM((inner, width), BF16),
            pltpu.VMEM((rows, 2 * inner), BF16),
            pltpu.SemaphoreType.DMA((shards * (2 + part // COLS) * (inner // COLS),)),
        ],
        compiler_params=params(40),
        cost_estimate=pl.CostEstimate(
            flops=10 * rows * width * inner,
            bytes_accessed=6 * width * inner + 6 * rows * width,
            transcendentals=rows * inner,
        ),
        name="expert_slots",
    )(rows_in, rows_grad, packed, low_up, back_low, up_in, up_out, down_in)


def adapter_grads(rows_in, rows_grad, hidden, grad_up, low_up, back_low, up_low, down_in):
    rows, width = rows_in.shape
    inner = hidden.shape[1]
    rank = up_low.shape[1]
    return pl.pallas_call(
        adapter_kernel,
        out_shape=jax.ShapeDtypeStruct((rank, 2 * (width + inner)), BF16),
        in_specs=[VMEM] * 8,
        out_specs=VMEM,
        compiler_params=params(24),
        cost_estimate=pl.CostEstimate(
            flops=4 * rows * rank * (width + inner),
            bytes_accessed=4 * rows * (width + inner),
            transcendentals=0,
        ),
        name="adapter_grads",
    )(rows_in, rows_grad, hidden, grad_up, low_up, back_low, up_low, down_in)


def replica_sum(own, axis):
    count = lax.axis_size(axis)
    total = own.astype(F32)
    for shift in range(1, count):
        pairs = [(i, (i + shift) % count) for i in range(count)]
        total += lax.ppermute(own, axis, pairs).astype(F32)
    return total


def on_device(
    tokens, out_grad, gate_prob, routes, limits,
    w_gate, w_up, w_down, up_in, up_out, down_in, down_out,
):
    width = tokens.shape[1]
    inner = up_out.shape[2]
    experts = limits.shape[0]
    slot_rows = experts * CAP
    packed = lax.all_gather(pack_weights(w_gate, w_up, w_down), "rep")
    send, slots = place_rows(routes, gate_prob, limits, tokens, out_grad)
    send = send.reshape(experts, 2 * CAP, width // LANES, LANES)
    recv = lax.all_to_all(send, ("grp", "exp"), split_axis=0, concat_axis=0, tiled=True)
    rows_in = recv[:, :CAP].reshape(slot_rows, width)
    rows_grad = recv[:, CAP:].reshape(slot_rows, width)
    low_up, back_low, up_in = low_products(rows_in, rows_grad, up_in, down_out)
    slot_grad, hidden, grad_up, up_low = expert_slots(
        rows_in, rows_grad, packed, low_up, back_low, up_in, up_out, down_in
    )
    adapters = replica_sum(
        adapter_grads(rows_in, rows_grad, hidden, grad_up, low_up, back_low, up_low, down_in), "rep"
    )
    back = lax.all_to_all(
        slot_grad.reshape(experts, CAP, width // LANES, LANES),
        ("grp", "exp"), split_axis=0, concat_axis=0, tiled=True,
    )
    token_grad = combine_rows(slots, back.reshape(slot_rows, width // LANES, LANES))
    return (
        token_grad.reshape(tokens.shape),
        adapters[None, :, 0:width],
        adapters[None, :, 2 * width : 2 * width + inner],
        adapters[None, :, 2 * width + inner :],
        adapters[None, :, width : 2 * width],
    )


def solution(mesh):
    rows = P(("rep", "grp", "exp"), None)
    owner = P(("grp", "exp"), None, None)
    return jax.shard_map(
        on_device,
        mesh=mesh,
        in_specs=(
            rows, rows, rows, rows, P(),
            P(("grp", "exp"), "rep", None),
            P(("grp", "exp"), "rep", None),
            P(("grp", "exp"), None, "rep"),
            owner, owner, owner, owner,
        ),
        out_specs=(rows, owner, owner, owner, owner),
        check_vma=False,
    )
```

```python
import jax
import jax.numpy as jnp
from jax import lax
from jax.experimental import pallas as pl
from jax.experimental.pallas import tpu as pltpu
from jax.sharding import PartitionSpec as P

CAP = 3
LANES = 128
COLS = 256
SCALE = 2.0
F32 = jnp.float32
BF16 = jnp.bfloat16

VMEM = pl.BlockSpec(memory_space=pltpu.VMEM)
SMEM = pl.BlockSpec(memory_space=pltpu.SMEM)
HBM = pl.BlockSpec(memory_space=pltpu.HBM)


def params(mib):
    return pltpu.CompilerParams(vmem_limit_bytes=mib * 1024 * 1024)


def place_kernel(routes, prob, limits, tokens, grads, send, slots, count, staged):
    total = send.shape[0]
    staged[...] = jnp.zeros_like(staged)

    def clear(e, carry):
        count[e] = 0
        return carry

    lax.fori_loop(0, limits.shape[0], clear, 0, unroll=8)

    def one_token(t, carry):
        row = tokens[t]
        grad = grads[t].astype(F32)
        for k in range(routes.shape[1]):
            e = routes[t, k]
            rank = count[e]
            count[e] = rank + 1
            kept = rank < limits[e]
            slots[t, k] = jnp.where(kept, e * CAP + rank, -1)
            place = jnp.where(kept, e * (2 * CAP) + rank, total)
            staged[place] = row
            staged[place + CAP] = (prob[t, k] * grad).astype(BF16)
        return carry

    lax.fori_loop(0, routes.shape[0], one_token, 0)
    send[...] = staged[0:total]


def place_rows(routes, prob, limits, tokens, grads):
    count, width = tokens.shape
    subs = width // LANES
    experts = limits.shape[0]
    total = experts * 2 * CAP
    return pl.pallas_call(
        place_kernel,
        out_shape=(
            jax.ShapeDtypeStruct((total, subs, LANES), BF16),
            jax.ShapeDtypeStruct(routes.shape, jnp.int32),
        ),
        in_specs=[SMEM, SMEM, SMEM, VMEM, VMEM],
        out_specs=(VMEM, SMEM),
        scratch_shapes=[
            pltpu.SMEM((experts,), jnp.int32),
            pltpu.VMEM((total + 2 * CAP, subs, LANES), BF16),
        ],
        compiler_params=params(16),
        name="place_rows",
    )(routes, prob, limits, tokens.reshape(count, subs, LANES), grads.reshape(count, subs, LANES))


def combine_kernel(slots, back, out):
    def one_token(t, carry):
        total = jnp.zeros(out.shape[1:], F32)
        for k in range(slots.shape[1]):
            slot = slots[t, k]
            row = back[jnp.maximum(slot, 0)].astype(F32)
            total += jnp.where(slot >= 0, row, 0.0)
        out[t] = total.astype(BF16)
        return carry

    lax.fori_loop(0, slots.shape[0], one_token, 0)


def combine_rows(slots, back):
    return pl.pallas_call(
        combine_kernel,
        out_shape=jax.ShapeDtypeStruct((slots.shape[0],) + back.shape[1:], BF16),
        in_specs=[SMEM, VMEM],
        out_specs=VMEM,
        compiler_params=params(16),
        name="combine_rows",
    )(slots, back)


def dot(left, right, left_dim, right_dim):
    return lax.dot_general(
        left, right, (((left_dim,), (right_dim,)), ((), ())), preferred_element_type=F32
    )


def low_kernel(rows_in, rows_grad, up_in, down_out, low_up, back_low, up_in_near):
    low_up[...] = dot(rows_in[...], up_in[0], 1, 1).astype(BF16)
    back_low[...] = dot(rows_grad[...], down_out[0], 1, 1).astype(BF16)
    up_in_near[...] = up_in[0]


def low_products(rows_in, rows_grad, up_in, down_out):
    rows, width = rows_in.shape
    rank = up_in.shape[1]
    return pl.pallas_call(
        low_kernel,
        out_shape=(
            jax.ShapeDtypeStruct((rows, rank), BF16),
            jax.ShapeDtypeStruct((rows, rank), BF16),
            jax.ShapeDtypeStruct((rank, width), BF16),
        ),
        in_specs=[VMEM] * 4,
        out_specs=(VMEM,) * 3,
        compiler_params=params(16),
        cost_estimate=pl.CostEstimate(
            flops=4 * rows * rank * width, bytes_accessed=4 * rows * width, transcendentals=0
        ),
        name="low_products",
    )(rows_in, rows_grad, up_in, down_out)


def pieces(mine, shards, own, left, right, top, bottom):
    across = lax.rem(mine + 2, shards)
    return (
        (mine, 0, own),
        (lax.rem(mine + shards - 1, shards), 0, left),
        (lax.rem(mine + 1, shards), 0, right),
        (across, 0, top),
        (across, top.shape[1], bottom),
    )


def slot_kernel(
    rank, rows_in, rows_grad, low_up, back_low, up_in, up_out, down_in, *refs
):
    gates, ups, downs = refs[0:5], refs[5:10], refs[10:15]
    slot_grad, hidden, grad_up, up_low, gate_up, down, grads, sems = refs[15:]
    width = gate_up.shape[0]
    inner = hidden.shape[1]
    part = gates[0].shape[1]
    shards = width // part
    chunks = inner // COLS
    mine = rank[0]
    steps = []
    number = 0
    for c in range(chunks):
        cols = pl.ds(c * COLS, COLS)
        moves = []
        for i, refs_of in enumerate((gates, ups)):
            for shard, first, ref in pieces(mine, shards, *refs_of):
                rows = ref.shape[1]
                place = pl.multiple_of(shard * part + first, rows)
                moves.append(
                    (ref.at[0, :, cols], gate_up.at[pl.ds(place, rows), pl.ds(i * inner + c * COLS, COLS)])
                )
        for shard, first, ref in pieces(mine, shards, *downs):
            low = max(c * COLS, first)
            high = min((c + 1) * COLS, first + ref.shape[1])
            if low < high:
                place = pl.multiple_of(shard * part, part)
                moves.append(
                    (
                        ref.at[0, pl.ds(low - first, high - low), :],
                        down.at[pl.ds(low, high - low), pl.ds(place, part)],
                    )
                )
        copies = []
        for source, target in moves:
            copies.append(pltpu.make_async_copy(source, target, sems.at[number]))
            number += 1
        steps.append(copies)
    for copies in steps:
        for copy in copies:
            copy.start()

    x = rows_in
    g = rows_grad
    for c in range(chunks):
        cols = pl.ds(c * COLS, COLS)
        later = pl.ds(inner + c * COLS, COLS)
        for copy in steps[c]:
            copy.wait()
        gate_pre = dot(x[...], gate_up[:, cols], 1, 0)
        up_sum = dot(x[...], gate_up[:, later], 1, 0) + SCALE * dot(low_up[...], up_out[0, :, cols], 1, 0)
        grad_hidden = dot(g[...], down[cols, :], 1, 1) + SCALE * dot(
            back_low[...], down_in[0, :, cols], 1, 0
        )
        sig = jax.nn.sigmoid(gate_pre)
        active = gate_pre * sig
        up_grad = (grad_hidden * active).astype(BF16)
        hidden[:, cols] = (active * up_sum).astype(BF16)
        grads[:, cols] = (
            grad_hidden * up_sum * sig * (1.0 + gate_pre * (1.0 - sig))
        ).astype(BF16)
        grads[:, later] = up_grad
        grad_up[:, cols] = up_grad
    up_low[...] = dot(grad_up[...], up_out[0], 1, 1).astype(BF16)
    for c in range(width // COLS):
        cols = pl.ds(c * COLS, COLS)
        slot_grad[:, cols] = (
            dot(grads[...], gate_up[cols, :], 1, 1) + SCALE * dot(up_low[...], up_in[:, cols], 1, 0)
        ).astype(BF16)


def adapter_kernel(rows_in, rows_grad, hidden, grad_up, low_up, back_low, up_low, down_in, adapters):
    width, inner = rows_in.shape[1], hidden.shape[1]
    low_down = dot(hidden[...], down_in[0], 1, 1).astype(BF16)
    at = 0
    for left, right in (
        (up_low[...], rows_in),
        (low_down, rows_grad),
        (low_up[...], grad_up),
        (back_low[...], hidden),
    ):
        for c in range(right.shape[1] // COLS):
            piece = dot(left, right[:, pl.ds(c * COLS, COLS)], 0, 0)
            adapters[:, pl.ds(at, COLS)] = (SCALE * piece).astype(BF16)
            at += COLS


def expert_slots(rows_in, rows_grad, gates, ups, downs, low_up, back_low, up_in, up_out, down_in):
    rows, width = rows_in.shape
    rank, inner = up_out.shape[1:]
    mine = lax.axis_index("rep").astype(jnp.int32).reshape(1)
    return pl.pallas_call(
        slot_kernel,
        out_shape=(
            jax.ShapeDtypeStruct((rows, width), BF16),
            jax.ShapeDtypeStruct((rows, inner), BF16),
            jax.ShapeDtypeStruct((rows, inner), BF16),
            jax.ShapeDtypeStruct((rows, rank), BF16),
        ),
        in_specs=[SMEM] + [VMEM] * 7 + [HBM] * 15,
        out_specs=(VMEM,) * 4,
        scratch_shapes=[
            pltpu.VMEM((width, 2 * inner), BF16),
            pltpu.VMEM((inner, width), BF16),
            pltpu.VMEM((rows, 2 * inner), BF16),
            pltpu.SemaphoreType.DMA((15 * (inner // COLS),)),
        ],
        compiler_params=params(40),
        cost_estimate=pl.CostEstimate(
            flops=10 * rows * width * inner,
            bytes_accessed=6 * width * inner + 6 * rows * width,
            transcendentals=rows * inner,
        ),
        name="expert_slots",
    )(mine, rows_in, rows_grad, low_up, back_low, up_in, up_out, down_in, *gates, *ups, *downs)


def adapter_grads(rows_in, rows_grad, hidden, grad_up, low_up, back_low, up_low, down_in):
    rows, width = rows_in.shape
    inner = hidden.shape[1]
    rank = up_low.shape[1]
    return pl.pallas_call(
        adapter_kernel,
        out_shape=jax.ShapeDtypeStruct((rank, 2 * (width + inner)), BF16),
        in_specs=[VMEM] * 8,
        out_specs=VMEM,
        compiler_params=params(24),
        cost_estimate=pl.CostEstimate(
            flops=4 * rows * rank * (width + inner),
            bytes_accessed=4 * rows * (width + inner),
            transcendentals=0,
        ),
        name="adapter_grads",
    )(rows_in, rows_grad, hidden, grad_up, low_up, back_low, up_low, down_in)


def shifted(value, axis, shift):
    count = lax.axis_size(axis)
    return lax.ppermute(value, axis, [(i, (i + shift) % count) for i in range(count)])


def replica_sum(own, axis):
    total = own.astype(F32)
    for shift in range(1, lax.axis_size(axis)):
        total += shifted(own, axis, shift).astype(F32)
    return total


def ring_gather(own, axis):
    half = own.shape[1] // 2
    left = shifted(own, axis, 1)
    right = shifted(own, axis, -1)
    return own, left, right, shifted(left[:, :half], axis, 1), shifted(right[:, half:], axis, -1)


def on_device(
    tokens, out_grad, gate_prob, routes, limits,
    w_gate, w_up, w_down, up_in, up_out, down_in, down_out,
):
    width = tokens.shape[1]
    inner = up_out.shape[2]
    experts = limits.shape[0]
    slot_rows = experts * CAP
    gates, ups, downs = (ring_gather(w, "rep") for w in (w_gate, w_up, w_down))
    send, slots = place_rows(routes, gate_prob, limits, tokens, out_grad)
    send = send.reshape(experts, 2 * CAP, width // LANES, LANES)
    recv = lax.all_to_all(send, ("grp", "exp"), split_axis=0, concat_axis=0, tiled=True)
    rows_in = recv[:, :CAP].reshape(slot_rows, width)
    rows_grad = recv[:, CAP:].reshape(slot_rows, width)
    low_up, back_low, up_in = low_products(rows_in, rows_grad, up_in, down_out)
    slot_grad, hidden, grad_up, up_low = expert_slots(
        rows_in, rows_grad, gates, ups, downs, low_up, back_low, up_in, up_out, down_in
    )
    adapters = replica_sum(
        adapter_grads(rows_in, rows_grad, hidden, grad_up, low_up, back_low, up_low, down_in), "rep"
    )
    back = lax.all_to_all(
        slot_grad.reshape(experts, CAP, width // LANES, LANES),
        ("grp", "exp"), split_axis=0, concat_axis=0, tiled=True,
    )
    token_grad = combine_rows(slots, back.reshape(slot_rows, width // LANES, LANES))
    return (
        token_grad.reshape(tokens.shape),
        adapters[None, :, 0:width],
        adapters[None, :, 2 * width : 2 * width + inner],
        adapters[None, :, 2 * width + inner :],
        adapters[None, :, width : 2 * width],
    )


def solution(mesh):
    rows = P(("rep", "grp", "exp"), None)
    owner = P(("grp", "exp"), None, None)
    return jax.shard_map(
        on_device,
        mesh=mesh,
        in_specs=(
            rows, rows, rows, rows, P(),
            P(("grp", "exp"), "rep", None),
            P(("grp", "exp"), "rep", None),
            P(("grp", "exp"), None, "rep"),
            owner, owner, owner, owner,
        ),
        out_specs=(rows, owner, owner, owner, owner),
        check_vma=False,
    )
```

```python
import jax
import jax.numpy as jnp
from jax import lax
from jax.experimental import pallas as pl
from jax.experimental.pallas import tpu as pltpu
from jax.sharding import PartitionSpec as P

CAP = 3
LANES = 128
COLS = 256
SCALE = 2.0
F32 = jnp.float32
BF16 = jnp.bfloat16

VMEM = pl.BlockSpec(memory_space=pltpu.VMEM)
SMEM = pl.BlockSpec(memory_space=pltpu.SMEM)
HBM = pl.BlockSpec(memory_space=pltpu.HBM)


def params(mib):
    return pltpu.CompilerParams(vmem_limit_bytes=mib * 1024 * 1024)


def block_rows(shapes):
    rows = []
    start = 0
    for weight, (height, cols) in enumerate(shapes):
        for c in range(cols // COLS):
            rows.append((weight, c, start, height))
            start += height
    return rows, start


def in_halves(first, last, half):
    parts = []
    for side in range(2):
        low = max(first, side * half)
        high = min(last, (side + 1) * half)
        if low < high:
            parts.append((side, low - side * half, low - first, high - low))
    return parts


def place_kernel(
    routes, prob, limits, tokens, grads, w_gate, w_up, w_down,
    send, slots, first_half, second_half,
    count, staged, token_rows, grad_rows, packed, sems,
):
    halves = (first_half, second_half)
    blocks, _ = block_rows([w.shape[1:] for w in (w_gate, w_up, w_down)])
    loads = []
    for i, (weight, c, start, height) in enumerate(blocks):
        ref = (w_gate, w_up, w_down)[weight]
        loads.append(
            pltpu.make_async_copy(
                ref.at[0, :, pl.ds(c * COLS, COLS)], packed.at[pl.ds(start, height), :], sems.at[i]
            )
        )
    for load in loads:
        load.start()

    total = send.shape[0]
    staged[...] = jnp.zeros_like(staged)
    token_rows[...] = tokens[...].reshape(token_rows.shape)
    grad_rows[...] = grads[...].reshape(grad_rows.shape)

    def clear(e, carry):
        count[e] = 0
        return carry

    lax.fori_loop(0, limits.shape[0], clear, 0, unroll=8)
    for load in loads:
        load.wait()
    half = packed.shape[0] // 2
    stores = [
        pltpu.make_async_copy(packed.at[pl.ds(i * half, half), :], halves[i], sems.at[len(blocks) + i])
        for i in range(2)
    ]
    for store in stores:
        store.start()

    def one_token(t, carry):
        row = token_rows[t]
        grad = grad_rows[t].astype(F32)
        for k in range(routes.shape[0]):
            e = routes[k, t]
            rank = count[e]
            count[e] = rank + 1
            kept = rank < limits[e]
            slots[k, t] = jnp.where(kept, e * CAP + rank, -1)
            place = jnp.where(kept, e * (2 * CAP) + rank, total)
            staged[place] = row
            staged[place + CAP] = (prob[k, t] * grad).astype(BF16)
        return carry

    lax.fori_loop(0, routes.shape[1], one_token, 0)
    send[...] = staged[0:total]
    for store in stores:
        store.wait()


def place_rows(routes, prob, limits, tokens, grads, w_gate, w_up, w_down):
    count, width = tokens.shape
    subs = width // LANES
    experts = limits.shape[0]
    total = experts * 2 * CAP
    blocks, rows = block_rows([w.shape[1:] for w in (w_gate, w_up, w_down)])
    return pl.pallas_call(
        place_kernel,
        out_shape=(
            jax.ShapeDtypeStruct((total, subs, LANES), BF16),
            jax.ShapeDtypeStruct(routes.shape, jnp.int32),
            jax.ShapeDtypeStruct((rows // 2, COLS), BF16),
            jax.ShapeDtypeStruct((rows // 2, COLS), BF16),
        ),
        in_specs=[SMEM, SMEM, SMEM, VMEM, VMEM, HBM, HBM, HBM],
        out_specs=(VMEM, SMEM, HBM, HBM),
        scratch_shapes=[
            pltpu.SMEM((experts,), jnp.int32),
            pltpu.VMEM((total + 2 * CAP, subs, LANES), BF16),
            pltpu.VMEM((count, subs, LANES), BF16),
            pltpu.VMEM((count, subs, LANES), BF16),
            pltpu.VMEM((rows, COLS), BF16),
            pltpu.SemaphoreType.DMA((len(blocks) + 2,)),
        ],
        compiler_params=params(56),
        name="place_rows",
    )(routes, prob, limits, tokens, grads, w_gate, w_up, w_down)


def combine_kernel(slots, back, out, rows):
    def one_token(t, carry):
        total = jnp.zeros(rows.shape[1:], F32)
        for k in range(slots.shape[0]):
            slot = slots[k, t]
            row = back[jnp.maximum(slot, 0)].astype(F32)
            total += jnp.where(slot >= 0, row, 0.0)
        rows[t] = total.astype(BF16)
        return carry

    lax.fori_loop(0, slots.shape[1], one_token, 0)
    out[...] = rows[...].reshape(out.shape)


def combine_rows(slots, back):
    count = slots.shape[1]
    subs, lanes = back.shape[1:]
    return pl.pallas_call(
        combine_kernel,
        out_shape=jax.ShapeDtypeStruct((count, subs * lanes), BF16),
        in_specs=[SMEM, VMEM],
        out_specs=VMEM,
        scratch_shapes=[pltpu.VMEM((count, subs, lanes), BF16)],
        compiler_params=params(16),
        name="combine_rows",
    )(slots, back)


def dot(left, right, left_dim, right_dim):
    return lax.dot_general(
        left, right, (((left_dim,), (right_dim,)), ((), ())), preferred_element_type=F32
    )


def low_kernel(recv, up_in, down_out, rows_in, rows_grad, low_up, back_low, up_in_near):
    x = recv[:, :CAP].reshape(rows_in.shape)
    rows_in[...] = x
    low_up[...] = dot(x, up_in[0], 1, 1).astype(BF16)
    g = recv[:, CAP:].reshape(rows_grad.shape)
    rows_grad[...] = g
    back_low[...] = dot(g, down_out[0], 1, 1).astype(BF16)
    up_in_near[...] = up_in[0]


def low_products(recv, up_in, down_out):
    rows = recv.shape[0] * CAP
    rank, width = up_in.shape[1:]
    return pl.pallas_call(
        low_kernel,
        out_shape=(
            jax.ShapeDtypeStruct((rows, width), BF16),
            jax.ShapeDtypeStruct((rows, width), BF16),
            jax.ShapeDtypeStruct((rows, rank), BF16),
            jax.ShapeDtypeStruct((rows, rank), BF16),
            jax.ShapeDtypeStruct((rank, width), BF16),
        ),
        in_specs=[VMEM] * 3,
        out_specs=(VMEM,) * 5,
        compiler_params=params(24),
        cost_estimate=pl.CostEstimate(
            flops=4 * rows * rank * width, bytes_accessed=8 * rows * width, transcendentals=0
        ),
        name="low_products",
    )(recv, up_in, down_out)


def slot_kernel(rank, rows_in, rows_grad, low_up, back_low, up_in, up_out, down_in, *refs):
    owners = (refs[0:2], refs[2:4], refs[4:6], refs[6:8])
    slot_grad, hidden, grad_up, up_low, gate_up, down, grads, slot_rows, sems = refs[8:]
    width = gate_up.shape[0]
    inner = hidden.shape[1]
    shards = len(owners)
    part = width // shards
    chunks = inner // COLS
    half = owners[0][0].shape[0]
    blocks, _ = block_rows([(part, inner), (part, inner), (inner, part)])
    mine = rank[0]
    shifts = (0, shards - 1, 1, 2)
    steps = []
    number = 0
    for c in range(chunks):
        moves = []
        for shift, pair in zip(shifts, owners):
            place = pl.multiple_of(lax.rem(mine + shift, shards) * part, part)
            for weight, block, start, height in blocks:
                if weight < 2 and block != c:
                    continue
                if weight == 2:
                    start, height = start + c * COLS, COLS
                for side, at, skip, rows in in_halves(start, start + height, half):
                    if weight < 2:
                        target = gate_up.at[
                            pl.ds(pl.multiple_of(place + skip, COLS), rows),
                            pl.ds(weight * inner + c * COLS, COLS),
                        ]
                    else:
                        target = down.at[
                            pl.ds(c * COLS + skip, rows),
                            pl.ds(pl.multiple_of(place + block * COLS, COLS), COLS),
                        ]
                    moves.append((pair[side].at[pl.ds(at, rows), :], target))
        copies = []
        for source, target in moves:
            copies.append(pltpu.make_async_copy(source, target, sems.at[number]))
            number += 1
        steps.append(copies)
    for copies in steps:
        for copy in copies:
            copy.start()

    x = rows_in
    g = rows_grad
    for c in range(chunks):
        cols = pl.ds(c * COLS, COLS)
        later = pl.ds(inner + c * COLS, COLS)
        for copy in steps[c]:
            copy.wait()
        gate_pre = dot(x[...], gate_up[:, cols], 1, 0)
        up_sum = dot(x[...], gate_up[:, later], 1, 0) + SCALE * dot(low_up[...], up_out[0, :, cols], 1, 0)
        grad_hidden = dot(g[...], down[cols, :], 1, 1) + SCALE * dot(
            back_low[...], down_in[0, :, cols], 1, 0
        )
        sig = jax.nn.sigmoid(gate_pre)
        active = gate_pre * sig
        up_grad = (grad_hidden * active).astype(BF16)
        hidden[:, cols] = (active * up_sum).astype(BF16)
        grads[:, cols] = (
            grad_hidden * up_sum * sig * (1.0 + gate_pre * (1.0 - sig))
        ).astype(BF16)
        grads[:, later] = up_grad
        grad_up[:, cols] = up_grad
    up_low[...] = dot(grad_up[...], up_out[0], 1, 1).astype(BF16)
    for c in range(width // COLS):
        cols = pl.ds(c * COLS, COLS)
        slot_rows[:, cols] = (
            dot(grads[...], gate_up[cols, :], 1, 1) + SCALE * dot(up_low[...], up_in[:, cols], 1, 0)
        ).astype(BF16)
    slot_grad[...] = slot_rows[...].reshape(slot_grad.shape)


def adapter_kernel(rows_in, rows_grad, hidden, grad_up, low_up, back_low, up_low, down_in, adapters):
    width, inner = rows_in.shape[1], hidden.shape[1]
    low_down = dot(hidden[...], down_in[0], 1, 1).astype(BF16)
    at = 0
    for left, right in (
        (up_low[...], rows_in),
        (low_down, rows_grad),
        (low_up[...], grad_up),
        (back_low[...], hidden),
    ):
        for c in range(right.shape[1] // COLS):
            piece = dot(left, right[:, pl.ds(c * COLS, COLS)], 0, 0)
            adapters[:, pl.ds(at, COLS)] = (SCALE * piece).astype(BF16)
            at += COLS


def expert_slots(rows_in, rows_grad, weights, low_up, back_low, up_in, up_out, down_in):
    rows, width = rows_in.shape
    rank, inner = up_out.shape[1:]
    mine = lax.axis_index("rep").astype(jnp.int32).reshape(1)
    return pl.pallas_call(
        slot_kernel,
        out_shape=(
            jax.ShapeDtypeStruct((rows, width // LANES, LANES), BF16),
            jax.ShapeDtypeStruct((rows, inner), BF16),
            jax.ShapeDtypeStruct((rows, inner), BF16),
            jax.ShapeDtypeStruct((rows, rank), BF16),
        ),
        in_specs=[SMEM] + [VMEM] * 7 + [HBM] * 8,
        out_specs=(VMEM,) * 4,
        scratch_shapes=[
            pltpu.VMEM((width, 2 * inner), BF16),
            pltpu.VMEM((inner, width), BF16),
            pltpu.VMEM((rows, 2 * inner), BF16),
            pltpu.VMEM((rows, width), BF16),
            pltpu.SemaphoreType.DMA((72,)),
        ],
        compiler_params=params(40),
        cost_estimate=pl.CostEstimate(
            flops=10 * rows * width * inner,
            bytes_accessed=6 * width * inner + 6 * rows * width,
            transcendentals=rows * inner,
        ),
        name="expert_slots",
    )(mine, rows_in, rows_grad, low_up, back_low, up_in, up_out, down_in, *weights)


def adapter_grads(rows_in, rows_grad, hidden, grad_up, low_up, back_low, up_low, down_in):
    rows, width = rows_in.shape
    inner = hidden.shape[1]
    rank = up_low.shape[1]
    return pl.pallas_call(
        adapter_kernel,
        out_shape=jax.ShapeDtypeStruct((rank, 2 * (width + inner)), BF16),
        in_specs=[VMEM] * 8,
        out_specs=VMEM,
        compiler_params=params(24),
        cost_estimate=pl.CostEstimate(
            flops=4 * rows * rank * (width + inner),
            bytes_accessed=4 * rows * (width + inner),
            transcendentals=0,
        ),
        name="adapter_grads",
    )(rows_in, rows_grad, hidden, grad_up, low_up, back_low, up_low, down_in)


def shifted(value, axis, shift):
    count = lax.axis_size(axis)
    return lax.ppermute(value, axis, [(i, (i + shift) % count) for i in range(count)])


def replica_sum(own, axis):
    total = own.astype(F32)
    for shift in range(1, lax.axis_size(axis)):
        total += shifted(own, axis, shift).astype(F32)
    return total


def ring_gather(first, second, axis):
    left_first = shifted(first, axis, 1)
    right_second = shifted(second, axis, -1)
    right_first = shifted(first, axis, -1)
    left_second = shifted(second, axis, 1)
    far_first = shifted(left_first, axis, 1)
    far_second = shifted(right_second, axis, -1)
    return first, second, left_first, left_second, right_first, right_second, far_first, far_second


def on_device(
    tokens, out_grad, gate_prob, routes, limits,
    w_gate, w_up, w_down, up_in, up_out, down_in, down_out,
):
    width = tokens.shape[1]
    inner = up_out.shape[2]
    experts = limits.shape[0]
    slot_rows = experts * CAP
    send, slots, *own = place_rows(
        routes.T, gate_prob.T, limits, tokens, out_grad, w_gate, w_up, w_down
    )
    weights = ring_gather(*own, "rep")
    recv = lax.all_to_all(
        send.reshape(experts, 2 * CAP, width // LANES, LANES),
        ("grp", "exp"), split_axis=0, concat_axis=0, tiled=True,
    )
    rows_in, rows_grad, low_up, back_low, up_in = low_products(recv, up_in, down_out)
    slot_grad, hidden, grad_up, up_low = expert_slots(
        rows_in, rows_grad, weights, low_up, back_low, up_in, up_out, down_in
    )
    adapters = replica_sum(
        adapter_grads(rows_in, rows_grad, hidden, grad_up, low_up, back_low, up_low, down_in), "rep"
    )
    back = lax.all_to_all(
        slot_grad.reshape(experts, CAP, width // LANES, LANES),
        ("grp", "exp"), split_axis=0, concat_axis=0, tiled=True,
    )
    token_grad = combine_rows(slots, back.reshape(slot_rows, width // LANES, LANES))
    return (
        token_grad,
        adapters[None, :, 0:width],
        adapters[None, :, 2 * width : 2 * width + inner],
        adapters[None, :, 2 * width + inner :],
        adapters[None, :, width : 2 * width],
    )


def solution(mesh):
    rows = P(("rep", "grp", "exp"), None)
    owner = P(("grp", "exp"), None, None)
    return jax.shard_map(
        on_device,
        mesh=mesh,
        in_specs=(
            rows, rows, rows, rows, P(),
            P(("grp", "exp"), "rep", None),
            P(("grp", "exp"), "rep", None),
            P(("grp", "exp"), None, "rep"),
            owner, owner, owner, owner,
        ),
        out_specs=(rows, owner, owner, owner, owner),
        check_vma=False,
    )
```

```python
import jax
import jax.numpy as jnp
from jax import lax
from jax.experimental import pallas as pl
from jax.experimental.pallas import tpu as pltpu
from jax.sharding import PartitionSpec as P

CAP = 3
LANES = 128
COLS = 256
ROW_STEPS = 4
SCALE = 2.0
F32 = jnp.float32
BF16 = jnp.bfloat16

VMEM = pl.BlockSpec(memory_space=pltpu.VMEM)
SMEM = pl.BlockSpec(memory_space=pltpu.SMEM)
HBM = pl.BlockSpec(memory_space=pltpu.HBM)


def params(mib):
    return pltpu.CompilerParams(vmem_limit_bytes=mib * 1024 * 1024)


def block_rows(shapes):
    rows = []
    start = 0
    for weight, (height, cols) in enumerate(shapes):
        for c in range(cols // COLS):
            rows.append((weight, c, start, height))
            start += height
    return rows, start


def in_halves(first, last, half):
    parts = []
    for side in range(2):
        low = max(first, side * half)
        high = min(last, (side + 1) * half)
        if low < high:
            parts.append((side, low - side * half, low - first, high - low))
    return parts


def place_kernel(
    routes, prob, limits, tokens, grads, w_gate, w_up, w_down,
    send, slots, first_half, second_half,
    count, staged, token_rows, grad_rows, packed, sems,
):
    halves = (first_half, second_half)
    blocks, _ = block_rows([w.shape[1:] for w in (w_gate, w_up, w_down)])
    loads = []
    for i, (weight, c, start, height) in enumerate(blocks):
        ref = (w_gate, w_up, w_down)[weight]
        loads.append(
            pltpu.make_async_copy(
                ref.at[0, :, pl.ds(c * COLS, COLS)], packed.at[pl.ds(start, height), :], sems.at[i]
            )
        )
    for load in loads:
        load.start()

    total = send.shape[0]
    staged[...] = jnp.zeros_like(staged)
    token_rows[...] = tokens[...].reshape(token_rows.shape)
    grad_rows[...] = grads[...].reshape(grad_rows.shape)

    def clear(e, carry):
        count[e] = 0
        return carry

    lax.fori_loop(0, limits.shape[0], clear, 0, unroll=8)
    for load in loads:
        load.wait()
    half = packed.shape[0] // 2
    stores = [
        pltpu.make_async_copy(packed.at[pl.ds(i * half, half), :], halves[i], sems.at[len(blocks) + i])
        for i in range(2)
    ]
    for store in stores:
        store.start()

    def one_token(t, carry):
        row = token_rows[t]
        grad = grad_rows[t].astype(F32)
        for k in range(routes.shape[0]):
            e = routes[k, t]
            rank = count[e]
            count[e] = rank + 1
            kept = rank < limits[e]
            slots[k, t] = jnp.where(kept, e * CAP + rank, -1)
            place = jnp.where(kept, e * (2 * CAP) + rank, total)
            staged[place] = row
            staged[place + CAP] = (prob[k, t] * grad).astype(BF16)
        return carry

    lax.fori_loop(0, routes.shape[1], one_token, 0)
    send[...] = staged[0:total]
    for store in stores:
        store.wait()


def place_rows(routes, prob, limits, tokens, grads, w_gate, w_up, w_down):
    count, width = tokens.shape
    subs = width // LANES
    experts = limits.shape[0]
    total = experts * 2 * CAP
    blocks, rows = block_rows([w.shape[1:] for w in (w_gate, w_up, w_down)])
    return pl.pallas_call(
        place_kernel,
        out_shape=(
            jax.ShapeDtypeStruct((total, subs, LANES), BF16),
            jax.ShapeDtypeStruct(routes.shape, jnp.int32),
            jax.ShapeDtypeStruct((rows // 2, COLS), BF16),
            jax.ShapeDtypeStruct((rows // 2, COLS), BF16),
        ),
        in_specs=[SMEM, SMEM, SMEM, VMEM, VMEM, HBM, HBM, HBM],
        out_specs=(VMEM, SMEM, HBM, HBM),
        scratch_shapes=[
            pltpu.SMEM((experts,), jnp.int32),
            pltpu.VMEM((total + 2 * CAP, subs, LANES), BF16),
            pltpu.VMEM((count, subs, LANES), BF16),
            pltpu.VMEM((count, subs, LANES), BF16),
            pltpu.VMEM((rows, COLS), BF16),
            pltpu.SemaphoreType.DMA((len(blocks) + 2,)),
        ],
        compiler_params=params(56),
        name="place_rows",
    )(routes, prob, limits, tokens, grads, w_gate, w_up, w_down)


def combine_kernel(slots, back, out, rows):
    def one_token(t, carry):
        total = jnp.zeros(rows.shape[1:], F32)
        for k in range(slots.shape[0]):
            slot = slots[k, t]
            row = back[jnp.maximum(slot, 0)].astype(F32)
            total += jnp.where(slot >= 0, row, 0.0)
        rows[t] = total.astype(BF16)
        return carry

    lax.fori_loop(0, slots.shape[1], one_token, 0)
    out[...] = rows[...].reshape(out.shape)


def combine_rows(slots, back):
    count = slots.shape[1]
    subs, lanes = back.shape[1:]
    return pl.pallas_call(
        combine_kernel,
        out_shape=jax.ShapeDtypeStruct((count, subs * lanes), BF16),
        in_specs=[SMEM, VMEM],
        out_specs=VMEM,
        scratch_shapes=[pltpu.VMEM((count, subs, lanes), BF16)],
        compiler_params=params(16),
        name="combine_rows",
    )(slots, back)


def dot(left, right, left_dim, right_dim):
    return lax.dot_general(
        left, right, (((left_dim,), (right_dim,)), ((), ())), preferred_element_type=F32
    )


def low_kernel(recv, up_in, down_out, rows_in, rows_grad, low_up, back_low, up_in_near):
    x = recv[:, :CAP].reshape(rows_in.shape)
    rows_in[...] = x
    low_up[...] = dot(x, up_in[0], 1, 1).astype(BF16)
    g = recv[:, CAP:].reshape(rows_grad.shape)
    rows_grad[...] = g
    back_low[...] = dot(g, down_out[0], 1, 1).astype(BF16)
    up_in_near[...] = up_in[0]


def low_products(recv, up_in, down_out):
    rows = recv.shape[0] * CAP
    rank, width = up_in.shape[1:]
    return pl.pallas_call(
        low_kernel,
        out_shape=(
            jax.ShapeDtypeStruct((rows, width), BF16),
            jax.ShapeDtypeStruct((rows, width), BF16),
            jax.ShapeDtypeStruct((rows, rank), BF16),
            jax.ShapeDtypeStruct((rows, rank), BF16),
            jax.ShapeDtypeStruct((rank, width), BF16),
        ),
        in_specs=[VMEM] * 3,
        out_specs=(VMEM,) * 5,
        compiler_params=params(24),
        cost_estimate=pl.CostEstimate(
            flops=4 * rows * rank * width, bytes_accessed=8 * rows * width, transcendentals=0
        ),
        name="low_products",
    )(recv, up_in, down_out)


def slot_kernel(rank, rows_in_far, rows_grad_far, low_up, back_low, up_in, up_out, down_in, *refs):
    owners = (refs[0:2], refs[2:4], refs[4:6], refs[6:8])
    slot_far, hidden_far, grad_up_far, up_low = refs[8:12]
    gate_up, down, grads, slot_rows, slot_grad, hidden, grad_up, x, g, sems, out_sems = refs[12:]
    width = gate_up.shape[0]
    inner = hidden.shape[1]
    shards = len(owners)
    part = width // shards
    chunks = inner // COLS
    half = owners[0][0].shape[0]
    blocks, _ = block_rows([(part, inner), (part, inner), (inner, part)])
    mine = rank[0]
    shifts = (0, shards - 1, 1, 2)
    steps = []
    number = 0
    for c in range(chunks):
        moves = ([], [])
        if c == 0:
            moves[0].append((rows_in_far, x))
            moves[1].append((rows_grad_far, g))
        for shift, pair in zip(shifts, owners):
            place = pl.multiple_of(lax.rem(mine + shift, shards) * part, part)
            for weight, block, start, height in blocks:
                if weight < 2 and block != c:
                    continue
                if weight == 2:
                    start, height = start + c * COLS, COLS
                for side, at, skip, rows in in_halves(start, start + height, half):
                    if weight < 2:
                        target = gate_up.at[
                            pl.ds(pl.multiple_of(place + skip, COLS), rows),
                            pl.ds(weight * inner + c * COLS, COLS),
                        ]
                    else:
                        target = down.at[
                            pl.ds(c * COLS + skip, rows),
                            pl.ds(pl.multiple_of(place + block * COLS, COLS), COLS),
                        ]
                    moves[weight // 2].append((pair[side].at[pl.ds(at, rows), :], target))
        for kind in moves:
            copies = []
            for source, target in kind:
                copies.append(pltpu.make_async_copy(source, target, sems.at[number]))
                number += 1
            steps.append(copies)
    for copies in steps:
        for copy in copies:
            copy.start()

    for c in range(chunks):
        cols = pl.ds(c * COLS, COLS)
        later = pl.ds(inner + c * COLS, COLS)
        for copy in steps[2 * c]:
            copy.wait()
        gate_pre = dot(x[...], gate_up[:, cols], 1, 0)
        up_sum = dot(x[...], gate_up[:, later], 1, 0) + SCALE * dot(low_up[...], up_out[0, :, cols], 1, 0)
        for copy in steps[2 * c + 1]:
            copy.wait()
        grad_hidden = dot(g[...], down[cols, :], 1, 1) + SCALE * dot(
            back_low[...], down_in[0, :, cols], 1, 0
        )
        sig = jax.nn.sigmoid(gate_pre)
        active = gate_pre * sig
        up_grad = (grad_hidden * active).astype(BF16)
        hidden[:, cols] = (active * up_sum).astype(BF16)
        grads[:, cols] = (
            grad_hidden * up_sum * sig * (1.0 + gate_pre * (1.0 - sig))
        ).astype(BF16)
        grads[:, later] = up_grad
        grad_up[:, cols] = up_grad
    stores = [
        pltpu.make_async_copy(hidden, hidden_far, out_sems.at[0]),
        pltpu.make_async_copy(grad_up, grad_up_far, out_sems.at[1]),
    ]
    for store in stores:
        store.start()
    up_low[...] = dot(grad_up[...], up_out[0], 1, 1).astype(BF16)
    for c in range(width // COLS):
        cols = pl.ds(c * COLS, COLS)
        slot_rows[:, cols] = (
            dot(grads[...], gate_up[cols, :], 1, 1) + SCALE * dot(up_low[...], up_in[:, cols], 1, 0)
        ).astype(BF16)
    step = slot_grad.shape[0] // ROW_STEPS
    for i in range(ROW_STEPS):
        rows = pl.ds(i * step, step)
        slot_grad[rows] = slot_rows[rows, :].reshape((step,) + slot_grad.shape[1:])
        store = pltpu.make_async_copy(slot_grad.at[rows], slot_far.at[rows], out_sems.at[2 + i])
        store.start()
        stores.append(store)
    for store in stores:
        store.wait()


def adapter_kernel(rows_in, rows_grad, hidden, grad_up, low_up, back_low, up_low, down_in, adapters):
    width, inner = rows_in.shape[1], hidden.shape[1]
    low_down = dot(hidden[...], down_in[0], 1, 1).astype(BF16)
    at = 0
    for left, right in (
        (up_low[...], rows_in),
        (low_down, rows_grad),
        (low_up[...], grad_up),
        (back_low[...], hidden),
    ):
        for c in range(right.shape[1] // COLS):
            piece = dot(left, right[:, pl.ds(c * COLS, COLS)], 0, 0)
            adapters[:, pl.ds(at, COLS)] = (SCALE * piece).astype(BF16)
            at += COLS


def expert_slots(rows_in, rows_grad, weights, low_up, back_low, up_in, up_out, down_in):
    rows, width = rows_in.shape
    rank, inner = up_out.shape[1:]
    mine = lax.axis_index("rep").astype(jnp.int32).reshape(1)
    return pl.pallas_call(
        slot_kernel,
        out_shape=(
            jax.ShapeDtypeStruct((rows, width // LANES, LANES), BF16),
            jax.ShapeDtypeStruct((rows, inner), BF16),
            jax.ShapeDtypeStruct((rows, inner), BF16),
            jax.ShapeDtypeStruct((rows, rank), BF16),
        ),
        in_specs=[SMEM, HBM, HBM] + [VMEM] * 5 + [HBM] * 8,
        out_specs=(HBM, HBM, HBM, VMEM),
        scratch_shapes=[
            pltpu.VMEM((width, 2 * inner), BF16),
            pltpu.VMEM((inner, width), BF16),
            pltpu.VMEM((rows, 2 * inner), BF16),
            pltpu.VMEM((rows, width), BF16),
            pltpu.VMEM((rows, width // LANES, LANES), BF16),
            pltpu.VMEM((rows, inner), BF16),
            pltpu.VMEM((rows, inner), BF16),
            pltpu.VMEM((rows, width), BF16),
            pltpu.VMEM((rows, width), BF16),
            pltpu.SemaphoreType.DMA((72,)),
            pltpu.SemaphoreType.DMA((2 + ROW_STEPS,)),
        ],
        compiler_params=params(57),
        cost_estimate=pl.CostEstimate(
            flops=10 * rows * width * inner,
            bytes_accessed=6 * width * inner + 6 * rows * width,
            transcendentals=rows * inner,
        ),
        name="expert_slots",
    )(mine, rows_in, rows_grad, low_up, back_low, up_in, up_out, down_in, *weights)


def adapter_grads(rows_in, rows_grad, hidden, grad_up, low_up, back_low, up_low, down_in):
    rows, width = rows_in.shape
    inner = hidden.shape[1]
    rank = up_low.shape[1]
    return pl.pallas_call(
        adapter_kernel,
        out_shape=jax.ShapeDtypeStruct((rank, 2 * (width + inner)), BF16),
        in_specs=[VMEM] * 8,
        out_specs=VMEM,
        compiler_params=params(24),
        cost_estimate=pl.CostEstimate(
            flops=4 * rows * rank * (width + inner),
            bytes_accessed=4 * rows * (width + inner),
            transcendentals=0,
        ),
        name="adapter_grads",
    )(rows_in, rows_grad, hidden, grad_up, low_up, back_low, up_low, down_in)


def shifted(value, axis, shift):
    count = lax.axis_size(axis)
    return lax.ppermute(value, axis, [(i, (i + shift) % count) for i in range(count)])


def replica_sum(own, axis):
    total = own.astype(F32)
    for shift in range(1, lax.axis_size(axis)):
        total += shifted(own, axis, shift).astype(F32)
    return total


def ring_gather(first, second, axis):
    left_first = shifted(first, axis, 1)
    right_second = shifted(second, axis, -1)
    right_first = shifted(first, axis, -1)
    left_second = shifted(second, axis, 1)
    far_first = shifted(left_first, axis, 1)
    far_second = shifted(right_second, axis, -1)
    return first, second, left_first, left_second, right_first, right_second, far_first, far_second


def on_device(
    tokens, out_grad, gate_prob, routes, limits,
    w_gate, w_up, w_down, up_in, up_out, down_in, down_out,
):
    width = tokens.shape[1]
    inner = up_out.shape[2]
    experts = limits.shape[0]
    slot_rows = experts * CAP
    send, slots, *own = place_rows(
        routes.T, gate_prob.T, limits, tokens, out_grad, w_gate, w_up, w_down
    )
    weights = ring_gather(*own, "rep")
    recv = lax.all_to_all(
        send.reshape(experts, 2 * CAP, width // LANES, LANES),
        ("grp", "exp"), split_axis=0, concat_axis=0, tiled=True,
    )
    rows_in, rows_grad, low_up, back_low, up_in = low_products(recv, up_in, down_out)
    slot_grad, hidden, grad_up, up_low = expert_slots(
        rows_in, rows_grad, weights, low_up, back_low, up_in, up_out, down_in
    )
    adapters = replica_sum(
        adapter_grads(rows_in, rows_grad, hidden, grad_up, low_up, back_low, up_low, down_in), "rep"
    )
    back = lax.all_to_all(
        slot_grad.reshape(experts, CAP, width // LANES, LANES),
        ("grp", "exp"), split_axis=0, concat_axis=0, tiled=True,
    )
    token_grad = combine_rows(slots, back.reshape(slot_rows, width // LANES, LANES))
    return (
        token_grad,
        adapters[None, :, 0:width],
        adapters[None, :, 2 * width : 2 * width + inner],
        adapters[None, :, 2 * width + inner :],
        adapters[None, :, width : 2 * width],
    )


def solution(mesh):
    rows = P(("rep", "grp", "exp"), None)
    owner = P(("grp", "exp"), None, None)
    return jax.shard_map(
        on_device,
        mesh=mesh,
        in_specs=(
            rows, rows, rows, rows, P(),
            P(("grp", "exp"), "rep", None),
            P(("grp", "exp"), "rep", None),
            P(("grp", "exp"), None, "rep"),
            owner, owner, owner, owner,
        ),
        out_specs=(rows, owner, owner, owner, owner),
        check_vma=False,
    )
```

```python
import jax
import jax.numpy as jnp
from jax import lax
from jax.experimental import pallas as pl
from jax.experimental.pallas import tpu as pltpu
from jax.sharding import PartitionSpec as P

CAP = 3
LANES = 128
COLS = 256
SCALE = 2.0
F32 = jnp.float32
BF16 = jnp.bfloat16

VMEM = pl.BlockSpec(memory_space=pltpu.VMEM)
SMEM = pl.BlockSpec(memory_space=pltpu.SMEM)
HBM = pl.BlockSpec(memory_space=pltpu.HBM)


def params(mib):
    return pltpu.CompilerParams(vmem_limit_bytes=mib * 1024 * 1024)


def block_rows(shapes):
    rows = []
    start = 0
    for weight, (height, cols) in enumerate(shapes):
        for c in range(cols // COLS):
            rows.append((weight, c, start, height))
            start += height
    return rows, start


def in_halves(first, last, half):
    parts = []
    for side in range(2):
        low = max(first, side * half)
        high = min(last, (side + 1) * half)
        if low < high:
            parts.append((side, low - side * half, low - first, high - low))
    return parts


def place_kernel(
    routes, prob, limits, tokens, grads, w_gate, w_up, w_down,
    send, slots, first_half, second_half,
    count, staged, token_rows, grad_rows, packed, sems,
):
    halves = (first_half, second_half)
    blocks, _ = block_rows([w.shape[1:] for w in (w_gate, w_up, w_down)])
    loads = []
    for i, (weight, c, start, height) in enumerate(blocks):
        ref = (w_gate, w_up, w_down)[weight]
        loads.append(
            pltpu.make_async_copy(
                ref.at[0, :, pl.ds(c * COLS, COLS)], packed.at[pl.ds(start, height), :], sems.at[i]
            )
        )
    for load in loads:
        load.start()

    total = send.shape[0]
    staged[...] = jnp.zeros_like(staged)
    token_rows[...] = tokens[...].reshape(token_rows.shape)
    grad_rows[...] = grads[...].reshape(grad_rows.shape)

    def clear(e, carry):
        count[e] = 0
        return carry

    lax.fori_loop(0, limits.shape[0], clear, 0, unroll=8)
    def one_token(t, carry):
        row = token_rows[t]
        grad = grad_rows[t].astype(F32)
        for k in range(routes.shape[0]):
            e = routes[k, t]
            rank = count[e]
            count[e] = rank + 1
            kept = rank < limits[e]
            slots[k, t] = jnp.where(kept, e * CAP + rank, -1)
            place = jnp.where(kept, e * (2 * CAP) + rank, total)
            staged[place] = row
            staged[place + CAP] = (prob[k, t] * grad).astype(BF16)
        return carry

    tokens_here = routes.shape[1]
    lax.fori_loop(0, tokens_here // 2, one_token, 0)
    for load in loads:
        load.wait()
    half = packed.shape[0] // 2
    stores = [
        pltpu.make_async_copy(packed.at[pl.ds(i * half, half), :], halves[i], sems.at[len(blocks) + i])
        for i in range(2)
    ]
    for store in stores:
        store.start()
    lax.fori_loop(tokens_here // 2, tokens_here, one_token, 0)
    send[...] = staged[0:total]
    for store in stores:
        store.wait()


def place_rows(routes, prob, limits, tokens, grads, w_gate, w_up, w_down):
    count, width = tokens.shape
    subs = width // LANES
    experts = limits.shape[0]
    total = experts * 2 * CAP
    blocks, rows = block_rows([w.shape[1:] for w in (w_gate, w_up, w_down)])
    return pl.pallas_call(
        place_kernel,
        out_shape=(
            jax.ShapeDtypeStruct((total, subs, LANES), BF16),
            jax.ShapeDtypeStruct(routes.shape, jnp.int32),
            jax.ShapeDtypeStruct((rows // 2, COLS), BF16),
            jax.ShapeDtypeStruct((rows // 2, COLS), BF16),
        ),
        in_specs=[SMEM, SMEM, SMEM, VMEM, VMEM, HBM, HBM, HBM],
        out_specs=(VMEM, SMEM, HBM, HBM),
        scratch_shapes=[
            pltpu.SMEM((experts,), jnp.int32),
            pltpu.VMEM((total + 2 * CAP, subs, LANES), BF16),
            pltpu.VMEM((count, subs, LANES), BF16),
            pltpu.VMEM((count, subs, LANES), BF16),
            pltpu.VMEM((rows, COLS), BF16),
            pltpu.SemaphoreType.DMA((len(blocks) + 2,)),
        ],
        compiler_params=params(56),
        name="place_rows",
    )(routes, prob, limits, tokens, grads, w_gate, w_up, w_down)


def combine_kernel(slots, back, out, rows):
    def one_token(t, carry):
        total = jnp.zeros(rows.shape[1:], F32)
        for k in range(slots.shape[0]):
            slot = slots[k, t]
            row = back[jnp.maximum(slot, 0)].astype(F32)
            total += jnp.where(slot >= 0, row, 0.0)
        rows[t] = total.astype(BF16)
        return carry

    lax.fori_loop(0, slots.shape[1], one_token, 0, unroll=2)
    out[...] = rows[...].reshape(out.shape)


def combine_rows(slots, back):
    count = slots.shape[1]
    subs, lanes = back.shape[1:]
    return pl.pallas_call(
        combine_kernel,
        out_shape=jax.ShapeDtypeStruct((count, subs * lanes), BF16),
        in_specs=[SMEM, VMEM],
        out_specs=VMEM,
        scratch_shapes=[pltpu.VMEM((count, subs, lanes), BF16)],
        compiler_params=params(16),
        name="combine_rows",
    )(slots, back)


def dot(left, right, left_dim, right_dim):
    return lax.dot_general(
        left, right, (((left_dim,), (right_dim,)), ((), ())), preferred_element_type=F32
    )


def low_kernel(recv, up_in, down_out, rows_in, rows_grad, low_up, back_low, up_in_near):
    x = recv[:, :CAP].reshape(rows_in.shape)
    rows_in[...] = x
    low_up[...] = dot(x, up_in[0], 1, 1).astype(BF16)
    g = recv[:, CAP:].reshape(rows_grad.shape)
    rows_grad[...] = g
    back_low[...] = dot(g, down_out[0], 1, 1).astype(BF16)
    up_in_near[...] = up_in[0]


def low_products(recv, up_in, down_out):
    rows = recv.shape[0] * CAP
    rank, width = up_in.shape[1:]
    return pl.pallas_call(
        low_kernel,
        out_shape=(
            jax.ShapeDtypeStruct((rows, width), BF16),
            jax.ShapeDtypeStruct((rows, width), BF16),
            jax.ShapeDtypeStruct((rows, rank), BF16),
            jax.ShapeDtypeStruct((rows, rank), BF16),
            jax.ShapeDtypeStruct((rank, width), BF16),
        ),
        in_specs=[VMEM] * 3,
        out_specs=(VMEM,) * 5,
        compiler_params=params(24),
        cost_estimate=pl.CostEstimate(
            flops=4 * rows * rank * width, bytes_accessed=8 * rows * width, transcendentals=0
        ),
        name="low_products",
    )(recv, up_in, down_out)


def slot_kernel(rank, rows_in, rows_grad, low_up, back_low, up_in, up_out, down_in, *refs):
    owners = (refs[0:2], refs[2:4], refs[4:6], refs[6:8])
    slot_grad, adapters, hidden, grad_up, up_low, gate_up, down, grads, slot_rows, sems = refs[8:]
    width = gate_up.shape[0]
    inner = hidden.shape[1]
    shards = len(owners)
    part = width // shards
    chunks = inner // COLS
    half = owners[0][0].shape[0]
    blocks, _ = block_rows([(part, inner), (part, inner), (inner, part)])
    mine = rank[0]
    shifts = (0, shards - 1, 1, 2)
    steps = []
    number = 0
    for c in range(chunks):
        moves = []
        for shift, pair in zip(shifts, owners):
            place = pl.multiple_of(lax.rem(mine + shift, shards) * part, part)
            for weight, block, start, height in blocks:
                if weight < 2 and block != c:
                    continue
                if weight == 2:
                    start, height = start + c * COLS, COLS
                for side, at, skip, rows in in_halves(start, start + height, half):
                    if weight < 2:
                        target = gate_up.at[
                            pl.ds(pl.multiple_of(place + skip, COLS), rows),
                            pl.ds(weight * inner + c * COLS, COLS),
                        ]
                    else:
                        target = down.at[
                            pl.ds(c * COLS + skip, rows),
                            pl.ds(pl.multiple_of(place + block * COLS, COLS), COLS),
                        ]
                    moves.append((pair[side].at[pl.ds(at, rows), :], target))
        copies = []
        for source, target in moves:
            copies.append(pltpu.make_async_copy(source, target, sems.at[number]))
            number += 1
        steps.append(copies)
    for copies in steps:
        for copy in copies:
            copy.start()

    x = rows_in
    g = rows_grad
    for c in range(chunks):
        cols = pl.ds(c * COLS, COLS)
        later = pl.ds(inner + c * COLS, COLS)
        for copy in steps[c]:
            copy.wait()
        gate_pre = dot(x[...], gate_up[:, cols], 1, 0)
        up_sum = dot(x[...], gate_up[:, later], 1, 0) + SCALE * dot(low_up[...], up_out[0, :, cols], 1, 0)
        grad_hidden = dot(g[...], down[cols, :], 1, 1) + SCALE * dot(
            back_low[...], down_in[0, :, cols], 1, 0
        )
        sig = jax.nn.sigmoid(gate_pre)
        active = gate_pre * sig
        up_grad = (grad_hidden * active).astype(BF16)
        hidden[:, cols] = (active * up_sum).astype(BF16)
        grads[:, cols] = (
            grad_hidden * up_sum * sig * (1.0 + gate_pre * (1.0 - sig))
        ).astype(BF16)
        grads[:, later] = up_grad
        grad_up[:, cols] = up_grad
    up_low[...] = dot(grad_up[...], up_out[0], 1, 1).astype(BF16)
    for c in range(width // COLS):
        cols = pl.ds(c * COLS, COLS)
        slot_rows[:, cols] = (
            dot(grads[...], gate_up[cols, :], 1, 1) + SCALE * dot(up_low[...], up_in[:, cols], 1, 0)
        ).astype(BF16)
    slot_grad[...] = slot_rows[...].reshape(slot_grad.shape)
    low_down = dot(hidden[...], down_in[0], 1, 1).astype(BF16)
    at = 0
    for left, right in (
        (up_low[...], x),
        (low_down, g),
        (low_up[...], grad_up),
        (back_low[...], hidden),
    ):
        for c in range(right.shape[1] // COLS):
            piece = dot(left, right[:, pl.ds(c * COLS, COLS)], 0, 0)
            adapters[:, pl.ds(at, COLS)] = (SCALE * piece).astype(BF16)
            at += COLS


def expert_slots(rows_in, rows_grad, weights, low_up, back_low, up_in, up_out, down_in):
    rows, width = rows_in.shape
    rank, inner = up_out.shape[1:]
    mine = lax.axis_index("rep").astype(jnp.int32).reshape(1)
    return pl.pallas_call(
        slot_kernel,
        out_shape=(
            jax.ShapeDtypeStruct((rows, width // LANES, LANES), BF16),
            jax.ShapeDtypeStruct((rank, 2 * (width + inner)), BF16),
        ),
        in_specs=[SMEM] + [VMEM] * 7 + [HBM] * 8,
        out_specs=(VMEM,) * 2,
        scratch_shapes=[
            pltpu.VMEM((rows, inner), BF16),
            pltpu.VMEM((rows, inner), BF16),
            pltpu.VMEM((rows, rank), BF16),
            pltpu.VMEM((width, 2 * inner), BF16),
            pltpu.VMEM((inner, width), BF16),
            pltpu.VMEM((rows, 2 * inner), BF16),
            pltpu.VMEM((rows, width), BF16),
            pltpu.SemaphoreType.DMA((72,)),
        ],
        compiler_params=params(40),
        cost_estimate=pl.CostEstimate(
            flops=10 * rows * width * inner,
            bytes_accessed=6 * width * inner + 6 * rows * width,
            transcendentals=rows * inner,
        ),
        name="expert_slots",
    )(mine, rows_in, rows_grad, low_up, back_low, up_in, up_out, down_in, *weights)


def shifted(value, axis, shift):
    count = lax.axis_size(axis)
    return lax.ppermute(value, axis, [(i, (i + shift) % count) for i in range(count)])


def replica_sum(own, axis):
    total = own.astype(F32)
    for shift in range(1, lax.axis_size(axis)):
        total += shifted(own, axis, shift).astype(F32)
    return total


def ring_gather(first, second, axis):
    left_first = shifted(first, axis, 1)
    right_second = shifted(second, axis, -1)
    right_first = shifted(first, axis, -1)
    left_second = shifted(second, axis, 1)
    far_first = shifted(left_first, axis, 1)
    far_second = shifted(right_second, axis, -1)
    return first, second, left_first, left_second, right_first, right_second, far_first, far_second


def on_device(
    tokens, out_grad, gate_prob, routes, limits,
    w_gate, w_up, w_down, up_in, up_out, down_in, down_out,
):
    width = tokens.shape[1]
    inner = up_out.shape[2]
    experts = limits.shape[0]
    slot_rows = experts * CAP
    send, slots, *own = place_rows(
        routes.T, gate_prob.T, limits, tokens, out_grad, w_gate, w_up, w_down
    )
    weights = ring_gather(*own, "rep")
    recv = lax.all_to_all(
        send.reshape(experts, 2 * CAP, width // LANES, LANES),
        ("grp", "exp"), split_axis=0, concat_axis=0, tiled=True,
    )
    rows_in, rows_grad, low_up, back_low, up_in = low_products(recv, up_in, down_out)
    slot_grad, adapters = expert_slots(
        rows_in, rows_grad, weights, low_up, back_low, up_in, up_out, down_in
    )
    adapters = replica_sum(adapters, "rep")
    back = lax.all_to_all(
        slot_grad.reshape(experts, CAP, width // LANES, LANES),
        ("grp", "exp"), split_axis=0, concat_axis=0, tiled=True,
    )
    token_grad = combine_rows(slots, back.reshape(slot_rows, width // LANES, LANES))
    return (
        token_grad,
        adapters[None, :, 0:width],
        adapters[None, :, 2 * width : 2 * width + inner],
        adapters[None, :, 2 * width + inner :],
        adapters[None, :, width : 2 * width],
    )


def solution(mesh):
    rows = P(("rep", "grp", "exp"), None)
    owner = P(("grp", "exp"), None, None)
    return jax.shard_map(
        on_device,
        mesh=mesh,
        in_specs=(
            rows, rows, rows, rows, P(),
            P(("grp", "exp"), "rep", None),
            P(("grp", "exp"), "rep", None),
            P(("grp", "exp"), None, "rep"),
            owner, owner, owner, owner,
        ),
        out_specs=(rows, owner, owner, owner, owner),
        check_vma=False,
    )
```

```python
import jax
import jax.numpy as jnp
from jax import lax
from jax.experimental import pallas as pl
from jax.experimental.pallas import tpu as pltpu
from jax.sharding import PartitionSpec as P

CAP = 3
LANES = 128
COLS = 256
ROW_STEPS = 4
SCALE = 2.0
F32 = jnp.float32
BF16 = jnp.bfloat16

VMEM = pl.BlockSpec(memory_space=pltpu.VMEM)
SMEM = pl.BlockSpec(memory_space=pltpu.SMEM)
HBM = pl.BlockSpec(memory_space=pltpu.HBM)


def params(mib):
    return pltpu.CompilerParams(vmem_limit_bytes=mib * 1024 * 1024)


def block_rows(shapes):
    rows = []
    start = 0
    for weight, (height, cols) in enumerate(shapes):
        for c in range(cols // COLS):
            rows.append((weight, c, start, height))
            start += height
    return rows, start


def in_halves(first, last, half):
    parts = []
    for side in range(2):
        low = max(first, side * half)
        high = min(last, (side + 1) * half)
        if low < high:
            parts.append((side, low - side * half, low - first, high - low))
    return parts


def place_kernel(
    routes, prob, limits, tokens, grads, w_gate, w_up, w_down,
    send, slots, first_half, second_half,
    count, staged, token_rows, grad_rows, packed, sems,
):
    halves = (first_half, second_half)
    blocks, _ = block_rows([w.shape[1:] for w in (w_gate, w_up, w_down)])
    loads = []
    for i, (weight, c, start, height) in enumerate(blocks):
        ref = (w_gate, w_up, w_down)[weight]
        loads.append(
            pltpu.make_async_copy(
                ref.at[0, :, pl.ds(c * COLS, COLS)], packed.at[pl.ds(start, height), :], sems.at[i]
            )
        )
    for load in loads:
        load.start()

    total = send.shape[0]
    staged[...] = jnp.zeros_like(staged)
    token_rows[...] = tokens[...].reshape(token_rows.shape)
    grad_rows[...] = grads[...].reshape(grad_rows.shape)

    def clear(e, carry):
        count[e] = 0
        return carry

    lax.fori_loop(0, limits.shape[0], clear, 0, unroll=8)
    def one_token(t, carry):
        row = token_rows[t]
        grad = grad_rows[t].astype(F32)
        for k in range(routes.shape[0]):
            e = routes[k, t]
            rank = count[e]
            count[e] = rank + 1
            kept = rank < limits[e]
            slots[k, t] = jnp.where(kept, e * CAP + rank, -1)
            place = jnp.where(kept, e * (2 * CAP) + rank, total)
            staged[place] = row
            staged[place + CAP] = (prob[k, t] * grad).astype(BF16)
        return carry

    tokens_here = routes.shape[1]
    lax.fori_loop(0, tokens_here // 2, one_token, 0)
    for load in loads:
        load.wait()
    half = packed.shape[0] // 2
    stores = [
        pltpu.make_async_copy(packed.at[pl.ds(i * half, half), :], halves[i], sems.at[len(blocks) + i])
        for i in range(2)
    ]
    for store in stores:
        store.start()
    lax.fori_loop(tokens_here // 2, tokens_here, one_token, 0)
    send[...] = staged[0:total]
    for store in stores:
        store.wait()


def place_rows(routes, prob, limits, tokens, grads, w_gate, w_up, w_down):
    count, width = tokens.shape
    subs = width // LANES
    experts = limits.shape[0]
    total = experts * 2 * CAP
    blocks, rows = block_rows([w.shape[1:] for w in (w_gate, w_up, w_down)])
    return pl.pallas_call(
        place_kernel,
        out_shape=(
            jax.ShapeDtypeStruct((total, subs, LANES), BF16),
            jax.ShapeDtypeStruct(routes.shape, jnp.int32),
            jax.ShapeDtypeStruct((rows // 2, COLS), BF16),
            jax.ShapeDtypeStruct((rows // 2, COLS), BF16),
        ),
        in_specs=[SMEM, SMEM, SMEM, VMEM, VMEM, HBM, HBM, HBM],
        out_specs=(VMEM, SMEM, HBM, HBM),
        scratch_shapes=[
            pltpu.SMEM((experts,), jnp.int32),
            pltpu.VMEM((total + 2 * CAP, subs, LANES), BF16),
            pltpu.VMEM((count, subs, LANES), BF16),
            pltpu.VMEM((count, subs, LANES), BF16),
            pltpu.VMEM((rows, COLS), BF16),
            pltpu.SemaphoreType.DMA((len(blocks) + 2,)),
        ],
        compiler_params=params(56),
        name="place_rows",
    )(routes, prob, limits, tokens, grads, w_gate, w_up, w_down)


def combine_kernel(slots, back, out, rows):
    def one_token(t, carry):
        total = jnp.zeros(rows.shape[1:], F32)
        for k in range(slots.shape[0]):
            slot = slots[k, t]
            row = back[jnp.maximum(slot, 0)].astype(F32)
            total += jnp.where(slot >= 0, row, 0.0)
        rows[t] = total.astype(BF16)
        return carry

    lax.fori_loop(0, slots.shape[1], one_token, 0, unroll=2)
    out[...] = rows[...].reshape(out.shape)


def combine_rows(slots, back):
    count = slots.shape[1]
    subs, lanes = back.shape[1:]
    return pl.pallas_call(
        combine_kernel,
        out_shape=jax.ShapeDtypeStruct((count, subs * lanes), BF16),
        in_specs=[SMEM, VMEM],
        out_specs=VMEM,
        scratch_shapes=[pltpu.VMEM((count, subs, lanes), BF16)],
        compiler_params=params(16),
        name="combine_rows",
    )(slots, back)


def dot(left, right, left_dim, right_dim):
    return lax.dot_general(
        left, right, (((left_dim,), (right_dim,)), ((), ())), preferred_element_type=F32
    )


def low_kernel(recv, up_in, down_out, rows_in, rows_grad, low_up, back_low, up_in_near):
    x = recv[:, :CAP].reshape(rows_in.shape)
    rows_in[...] = x
    low_up[...] = dot(x, up_in[0], 1, 1).astype(BF16)
    g = recv[:, CAP:].reshape(rows_grad.shape)
    rows_grad[...] = g
    back_low[...] = dot(g, down_out[0], 1, 1).astype(BF16)
    up_in_near[...] = up_in[0]


def low_products(recv, up_in, down_out):
    rows = recv.shape[0] * CAP
    rank, width = up_in.shape[1:]
    return pl.pallas_call(
        low_kernel,
        out_shape=(
            jax.ShapeDtypeStruct((rows, width), BF16),
            jax.ShapeDtypeStruct((rows, width), BF16),
            jax.ShapeDtypeStruct((rows, rank), BF16),
            jax.ShapeDtypeStruct((rows, rank), BF16),
            jax.ShapeDtypeStruct((rank, width), BF16),
        ),
        in_specs=[VMEM] * 3,
        out_specs=(VMEM,) * 5,
        compiler_params=params(24),
        cost_estimate=pl.CostEstimate(
            flops=4 * rows * rank * width, bytes_accessed=8 * rows * width, transcendentals=0
        ),
        name="low_products",
    )(recv, up_in, down_out)


def slot_kernel(rank, rows_in, rows_grad, low_up, back_low, up_in, up_out, down_in, *refs):
    owners = (refs[0:2], refs[2:4], refs[4:6], refs[6:8])
    slot_far, adapters, hidden, grad_up, up_low, gate_up, down, grads, slot_rows, slot_grad, sems, out_sems = refs[8:]
    width = gate_up.shape[0]
    inner = hidden.shape[1]
    shards = len(owners)
    part = width // shards
    chunks = inner // COLS
    half = owners[0][0].shape[0]
    blocks, _ = block_rows([(part, inner), (part, inner), (inner, part)])
    mine = rank[0]
    shifts = (0, shards - 1, 1, 2)
    steps = []
    number = 0
    for c in range(chunks):
        moves = []
        for shift, pair in zip(shifts, owners):
            place = pl.multiple_of(lax.rem(mine + shift, shards) * part, part)
            for weight, block, start, height in blocks:
                if weight < 2 and block != c:
                    continue
                if weight == 2:
                    start, height = start + c * COLS, COLS
                for side, at, skip, rows in in_halves(start, start + height, half):
                    if weight < 2:
                        target = gate_up.at[
                            pl.ds(pl.multiple_of(place + skip, COLS), rows),
                            pl.ds(weight * inner + c * COLS, COLS),
                        ]
                    else:
                        target = down.at[
                            pl.ds(c * COLS + skip, rows),
                            pl.ds(pl.multiple_of(place + block * COLS, COLS), COLS),
                        ]
                    moves.append((pair[side].at[pl.ds(at, rows), :], target))
        copies = []
        for source, target in moves:
            copies.append(pltpu.make_async_copy(source, target, sems.at[number]))
            number += 1
        steps.append(copies)
    for copies in steps:
        for copy in copies:
            copy.start()

    x = rows_in
    g = rows_grad
    for c in range(chunks):
        cols = pl.ds(c * COLS, COLS)
        later = pl.ds(inner + c * COLS, COLS)
        for copy in steps[c]:
            copy.wait()
        gate_pre = dot(x[...], gate_up[:, cols], 1, 0)
        up_sum = dot(x[...], gate_up[:, later], 1, 0) + SCALE * dot(low_up[...], up_out[0, :, cols], 1, 0)
        grad_hidden = dot(g[...], down[cols, :], 1, 1) + SCALE * dot(
            back_low[...], down_in[0, :, cols], 1, 0
        )
        sig = jax.nn.sigmoid(gate_pre)
        active = gate_pre * sig
        up_grad = (grad_hidden * active).astype(BF16)
        hidden[:, cols] = (active * up_sum).astype(BF16)
        grads[:, cols] = (
            grad_hidden * up_sum * sig * (1.0 + gate_pre * (1.0 - sig))
        ).astype(BF16)
        grads[:, later] = up_grad
        grad_up[:, cols] = up_grad
    up_low[...] = dot(grad_up[...], up_out[0], 1, 1).astype(BF16)
    for c in range(width // COLS):
        cols = pl.ds(c * COLS, COLS)
        slot_rows[:, cols] = (
            dot(grads[...], gate_up[cols, :], 1, 1) + SCALE * dot(up_low[...], up_in[:, cols], 1, 0)
        ).astype(BF16)
    step = slot_grad.shape[0] // ROW_STEPS
    stores = []
    for i in range(ROW_STEPS):
        rows = pl.ds(i * step, step)
        slot_grad[rows] = slot_rows[rows, :].reshape((step,) + slot_grad.shape[1:])
        stores.append(pltpu.make_async_copy(slot_grad.at[rows], slot_far.at[rows], out_sems.at[i]))
        stores[i].start()
    low_down = dot(hidden[...], down_in[0], 1, 1).astype(BF16)
    at = 0
    for left, right in (
        (up_low[...], x),
        (low_down, g),
        (low_up[...], grad_up),
        (back_low[...], hidden),
    ):
        for c in range(right.shape[1] // COLS):
            piece = dot(left, right[:, pl.ds(c * COLS, COLS)], 0, 0)
            adapters[:, pl.ds(at, COLS)] = (SCALE * piece).astype(BF16)
            at += COLS
    for store in stores:
        store.wait()


def expert_slots(rows_in, rows_grad, weights, low_up, back_low, up_in, up_out, down_in):
    rows, width = rows_in.shape
    rank, inner = up_out.shape[1:]
    mine = lax.axis_index("rep").astype(jnp.int32).reshape(1)
    return pl.pallas_call(
        slot_kernel,
        out_shape=(
            jax.ShapeDtypeStruct((rows, width // LANES, LANES), BF16),
            jax.ShapeDtypeStruct((rank, 2 * (width + inner)), BF16),
        ),
        in_specs=[SMEM] + [VMEM] * 7 + [HBM] * 8,
        out_specs=(HBM, VMEM),
        scratch_shapes=[
            pltpu.VMEM((rows, inner), BF16),
            pltpu.VMEM((rows, inner), BF16),
            pltpu.VMEM((rows, rank), BF16),
            pltpu.VMEM((width, 2 * inner), BF16),
            pltpu.VMEM((inner, width), BF16),
            pltpu.VMEM((rows, 2 * inner), BF16),
            pltpu.VMEM((rows, width), BF16),
            pltpu.VMEM((rows, width // LANES, LANES), BF16),
            pltpu.SemaphoreType.DMA((72,)),
            pltpu.SemaphoreType.DMA((ROW_STEPS,)),
        ],
        compiler_params=params(40),
        cost_estimate=pl.CostEstimate(
            flops=10 * rows * width * inner,
            bytes_accessed=6 * width * inner + 6 * rows * width,
            transcendentals=rows * inner,
        ),
        name="expert_slots",
    )(mine, rows_in, rows_grad, low_up, back_low, up_in, up_out, down_in, *weights)


def shifted(value, axis, shift):
    count = lax.axis_size(axis)
    return lax.ppermute(value, axis, [(i, (i + shift) % count) for i in range(count)])


def replica_sum(own, axis):
    total = own.astype(F32)
    for shift in range(1, lax.axis_size(axis)):
        total += shifted(own, axis, shift).astype(F32)
    return total


def ring_gather(first, second, axis):
    left_first = shifted(first, axis, 1)
    right_second = shifted(second, axis, -1)
    right_first = shifted(first, axis, -1)
    left_second = shifted(second, axis, 1)
    far_first = shifted(left_first, axis, 1)
    far_second = shifted(right_second, axis, -1)
    return first, second, left_first, left_second, right_first, right_second, far_first, far_second


def on_device(
    tokens, out_grad, gate_prob, routes, limits,
    w_gate, w_up, w_down, up_in, up_out, down_in, down_out,
):
    width = tokens.shape[1]
    inner = up_out.shape[2]
    experts = limits.shape[0]
    slot_rows = experts * CAP
    send, slots, *own = place_rows(
        routes.T, gate_prob.T, limits, tokens, out_grad, w_gate, w_up, w_down
    )
    weights = ring_gather(*own, "rep")
    recv = lax.all_to_all(
        send.reshape(experts, 2 * CAP, width // LANES, LANES),
        ("grp", "exp"), split_axis=0, concat_axis=0, tiled=True,
    )
    rows_in, rows_grad, low_up, back_low, up_in = low_products(recv, up_in, down_out)
    slot_grad, adapters = expert_slots(
        rows_in, rows_grad, weights, low_up, back_low, up_in, up_out, down_in
    )
    adapters = replica_sum(adapters, "rep")
    back = lax.all_to_all(
        slot_grad.reshape(experts, CAP, width // LANES, LANES),
        ("grp", "exp"), split_axis=0, concat_axis=0, tiled=True,
    )
    token_grad = combine_rows(slots, back.reshape(slot_rows, width // LANES, LANES))
    return (
        token_grad,
        adapters[None, :, 0:width],
        adapters[None, :, 2 * width : 2 * width + inner],
        adapters[None, :, 2 * width + inner :],
        adapters[None, :, width : 2 * width],
    )


def solution(mesh):
    rows = P(("rep", "grp", "exp"), None)
    owner = P(("grp", "exp"), None, None)
    return jax.shard_map(
        on_device,
        mesh=mesh,
        in_specs=(
            rows, rows, rows, rows, P(),
            P(("grp", "exp"), "rep", None),
            P(("grp", "exp"), "rep", None),
            P(("grp", "exp"), None, "rep"),
            owner, owner, owner, owner,
        ),
        out_specs=(rows, owner, owner, owner, owner),
        check_vma=False,
    )
```
